128 devices in a mesh: row: 8 (over y, z_hi), col: 16 (over x, z_lo, core).
Axes of the slice: x: 4, y: 4, z: 4 (z_hi: 2, z_lo: 2; z = z_hi * 2 + z_lo), core: 2. Of those that a mesh axis runs over, the one named last changes fastest.
Arguments:
- integrals: bfloat16 [8192, 8192], P('row', 'col'), may hold values from -0.0625 to 0.0625
- amplitudes: bfloat16 [8192, 8192], P('row', 'col'), may hold values from -6 to 6
- integral_tiles: int32 [64, 64], P('row', 'col'), may hold values 0 or 1
- amplitude_tiles: int32 [64, 64], P('row', 'col'), may hold values 0 or 1
- targets: int32 [64, 64], P('row', 'col'), may hold values from 0 to 511, as said below
Outputs:
- owned: bfloat16 [8, 512, 128, 128], P('row', 'col')
The draws below stay inside these ranges and needn't reach their ends.
Inputs may be any that keep to these rules, and one draw needn't show every extreme that they name: Within each mesh row the targets of the row's tiles are a permutation of 0 to 511. The tiles of one device go to at most 3 slots of any one block of 32 slots, and to exactly 3 slots of some block, in every row.
All inputs are finite; a program needn't handle non-finite values. No bound on the sum of `integral_tiles` or of `amplitude_tiles` on one device may be relied on, other than what follows from the above.
Results may differ from the reference program's by a relative error of at most 0.001.
Values may be sent and summed in bfloat16 or wider, within the bound.
A program may use at most 128 MiB of HBM per device.

```python
import jax
import jax.numpy as jnp
from jax import lax

TILE = 128
AT_DEV = 8
OT_DEV = 4
VPAIRS = 8192
OPAIRS = 8192
CONTRACT = 8192
TILES_DEV = 32
N_ROW = 8
N_COL = 16


def draw_targets(key, part):
    key = jax.random.fold_in(key, 7)
    tiles_dev = AT_DEV * OT_DEV
    base_count = tiles_dev // N_COL
    extra_count = tiles_dev - base_count * N_COL
    row_keys = jax.random.split(key, N_ROW)

    def one_row(row_key):
        keys_three = jax.random.split(row_key, 3)
        offset_order = jax.random.permutation(keys_three[0], N_COL)
        position = jnp.argsort(offset_order).astype(jnp.int32)
        counts = base_count + (position == 0).astype(jnp.int32) + ((position >= 1) & (position <= extra_count)).astype(jnp.int32) - (position == N_COL - 1).astype(jnp.int32)
        bounds = jnp.cumsum(counts)
        indices = jnp.arange(tiles_dev, dtype=jnp.int32)
        sorted_offsets = jnp.sum((bounds[None, :] <= indices[:, None]).astype(jnp.int32), axis=1)
        shuffle = jax.random.permutation(keys_three[1], tiles_dev)
        offsets = sorted_offsets[shuffle]
        columns = jnp.arange(N_COL, dtype=jnp.int32)
        target_col = (columns[:, None] + offsets[None, :]) % N_COL
        slot_keys = jax.random.split(keys_three[2], N_COL)
        slot_perms = jax.vmap(lambda one_key: jax.random.permutation(one_key, tiles_dev))(slot_keys)
        slots = slot_perms[target_col, indices[None, :]]
        return (target_col * tiles_dev + slots).astype(jnp.int32)
    table = jax.vmap(one_row)(row_keys)
    table = table.reshape(N_ROW, N_COL, AT_DEV, OT_DEV).transpose(0, 2, 1, 3)
    return table.reshape(N_ROW * AT_DEV, N_COL * OT_DEV).astype(jnp.int32)


def plant(result, own_key, least, high):
    dims = result.shape
    index_at = [jax.random.randint(jax.random.fold_in(own_key, axis), (), 0, dims[axis]) for axis in range(len(dims))]
    result = result.at[tuple(index_at)].set(least)
    longest = dims.index(max(dims))
    index_at[longest] = (index_at[longest] + 1) % dims[longest]
    return result.at[tuple(index_at)].set(high)


def levels(stream_key, shape, cuts, least, largest):
    factor_of = 1.0
    for axis_at, shards_of in cuts:
        heights = jax.random.uniform(jax.random.fold_in(jax.random.fold_in(stream_key, 6), axis_at), (shards_of,), jnp.float32, least / len(cuts), largest / len(cuts))
        factor_of = factor_of * jnp.repeat(jnp.exp(heights), shape[axis_at] // shards_of).reshape((-1,) + (1,) * (len(shape) - 1 - axis_at))
    return factor_of


def noise(own_key, extent, spread, limit, cuts=(), kind=jnp.bfloat16):
    loudness = levels(own_key, extent, cuts, -0.22, 0.18) if cuts else 1.0
    array = jax.random.normal(own_key, extent, jnp.float32) * spread * loudness
    return jnp.minimum(jnp.maximum(array, -limit), limit).astype(kind)


def setup_inputs(seed: int = 0) -> dict:
    keys = jax.random.split(jax.random.key(seed), 6)
    return {
        "integrals": noise(keys[0], (VPAIRS, CONTRACT), CONTRACT ** -0.5, 0.0625, ((0, 8), (1, 16))),
        "amplitudes": noise(keys[1], (CONTRACT, OPAIRS), 1.0, 6.0, ((0, 8), (1, 16))),
        "integral_tiles": plant((jax.random.randint(keys[2], (AT_DEV * N_ROW, AT_DEV * N_ROW), 0, 4) < 3).astype(jnp.int32), jax.random.fold_in(keys[2], 1), 0, 1),
        "amplitude_tiles": plant((jax.random.randint(keys[3], (AT_DEV * N_ROW, OT_DEV * N_COL), 0, 4) < 3).astype(jnp.int32), jax.random.fold_in(keys[3], 1), 0, 1),
        "targets": draw_targets(jax.random.fold_in(keys[5], 71), 0),
    }


def expand_mask(tiles, like):
    return jnp.repeat(jnp.repeat(tiles, TILE, axis=0), TILE, axis=1).astype(like.dtype)


def reference(integrals, amplitudes, integral_tiles, amplitude_tiles, targets):
    masked_integrals = integrals * expand_mask(integral_tiles, integrals)
    masked_amplitudes = amplitudes * expand_mask(amplitude_tiles, amplitudes)
    blocks = masked_integrals.reshape(N_ROW, AT_DEV * TILE, CONTRACT)
    row_targets = targets.reshape(N_ROW, AT_DEV * OT_DEV * N_COL)

    def one_row(pair):
        block, where = pair
        ladder = jnp.dot(block, masked_amplitudes, preferred_element_type=jnp.float32).astype(jnp.bfloat16)
        pieces = ladder.reshape(AT_DEV, TILE, OT_DEV * N_COL, TILE).transpose(0, 2, 1, 3)
        pieces = pieces.reshape(AT_DEV * OT_DEV * N_COL, TILE, TILE)
        owned_row = jnp.zeros((N_COL * TILES_DEV, TILE, TILE), jnp.bfloat16)
        return owned_row.at[where].set(pieces)

    return lax.map(one_row, (blocks, row_targets))
```

```python
import functools

import jax
import jax.numpy as jnp
from jax import lax
from jax.experimental import pallas as pl
from jax.experimental.pallas import tpu as pltpu
from jax.sharding import PartitionSpec as P

MESH = pl.DeviceIdType.MESH
T = 128
CAP = 3
PIECES = 4
PARTS = 2


class Sems:
    def __init__(self, ref):
        self.ref, self.used = ref, 0

    def take(self):
        self.used += 1
        return self.ref.at[self.used - 1]


def kernel(
    a_ref, b_ref, a_tiles, b_tiles, targets, out_ref,
    a_all, b_all, total, tiles, packed_parts, arrived_parts, label_out, label_in, table, table_s,
    send_ref, recv_a, recv_s, recv_b, recv_l, recv_d, local_sem,
):
    row, col = lax.axis_index("row"), lax.axis_index("col")
    y, zh = row // 2, row % 2
    x, zl, core = col // 4, (col // 2) % 2, col % 2
    sends = Sems(send_ref)
    started = []

    def col_of(dx, dv, dc):
        return lax.rem(x + dx + 4, 4) * 4 + lax.rem(zl + dv, 2) * 2 + lax.rem(core + dc, 2)

    def row_of(dy, dv):
        return lax.rem(y + dy + 4, 4) * 2 + lax.rem(zh + dv, 2)

    def send(src, dst, recv_sem, device):
        copy = pltpu.make_async_remote_copy(
            src_ref=src, dst_ref=dst, send_sem=sends.take(), recv_sem=recv_sem,
            device_id=device, device_id_type=MESH,
        )
        copy.start()
        started.append(copy)

    def landed(dst, recv_sem, device):
        pltpu.make_async_remote_copy(
            src_ref=dst, dst_ref=dst, send_sem=send_ref.at[0], recv_sem=recv_sem,
            device_id=device, device_id_type=MESH,
        ).wait_recv()

    barrier = pltpu.get_barrier_semaphore()
    peers = [(row, lax.rem(col + d, 16)) for d in range(1, 16)]
    peers += [(row_of(1, 0), col), (row_of(-1, 0), col), (row_of(0, 1), col)]
    for peer in peers:
        pl.semaphore_signal(barrier, inc=1, device_id=peer, device_id_type=MESH)

    rows_p = 8 // PIECES

    def mask(src, tile_flags, dst, p):
        for i in range(p * rows_p, (p + 1) * rows_p):
            for j in range(4):
                flag = tile_flags[i, j].astype(jnp.float32)
                block = src[pl.ds(i * T, T), pl.ds(j * T, T)].astype(jnp.float32) * flag
                dst[i, :, pl.ds(j * T, T)] = block.astype(jnp.bfloat16)

    mine_a = a_all.at[col]
    mine_b = b_all.at[row]
    mask(a_ref, a_tiles, mine_a, 0)
    mask(b_ref, b_tiles, mine_b, 0)
    pl.semaphore_wait(barrier, len(peers))

    def a_piece(dx, dv, dc, p):
        return a_all.at[col_of(-dx, dv, dc), pl.ds(p * rows_p, rows_p)]

    def b_piece(dy, dv, p):
        return b_all.at[row_of(-dy, dv), pl.ds(p * rows_p, rows_p)]

    def send_a(dx, dv, p, how):
        piece = a_piece(dx, dv, 0, p)
        if how == "right":
            send(piece, piece, recv_a.at[dx + 1, dv, p], (row, col_of(1, 0, 0)))
        elif how == "left":
            send(piece, piece, recv_a.at[(dx + 3) % 4, dv, p], (row, col_of(-1, 0, 0)))
        elif how == "z":
            send(piece, piece, recv_a.at[dx, 1 - dv, p], (row, col_of(0, 1, 0)))
        else:
            send(piece, piece, recv_s.at[dx, dv, p], (row, col_of(0, 0, 1)))

    def send_b(dy, dv, p, how):
        piece = b_piece(dy, dv, p)
        if how == "right":
            send(piece, piece, recv_b.at[dy + 1, dv, p], (row_of(1, 0), col))
        elif how == "left":
            send(piece, piece, recv_b.at[(dy + 3) % 4, dv, p], (row_of(-1, 0), col))
        else:
            send(piece, piece, recv_b.at[dy, 1 - dv, p], (row_of(0, 1), col))

    def got_a(dx, dv, p):
        landed(a_piece(dx, dv, 0, p), recv_a.at[dx, dv, p], (row, col_of(0, 1, 0)))

    def got_s(dx, dv, p):
        landed(a_piece(dx, dv, 1, p), recv_s.at[dx, dv, p], (row, col_of(0, 0, 1)))

    def got_b(dy, dv, p):
        landed(b_piece(dy, dv, p), recv_b.at[dy, dv, p], (row_of(0, 1), col))

    for p in range(PIECES):
        if p:
            mask(a_ref, a_tiles, mine_a, p)
        for how in ("z", "left", "right"):
            send_a(0, 0, p, how)
        if p:
            mask(b_ref, b_tiles, mine_b, p)
        for how in ("z", "left", "right"):
            send_b(0, 0, p, how)
    for p in range(PIECES):
        send_a(0, 0, p, "core")

    lane = lax.broadcasted_iota(jnp.int32, (8, 128), 1)
    lane16 = lax.broadcasted_iota(jnp.int32, (16, 8, 128), 2)
    owner16 = lax.broadcasted_iota(jnp.int32, (16, 8, 128), 0)

    def place(t, carry):
        source, label = carry
        target = targets[t // 4, lax.rem(t, 4)]
        owner, slot = target // 32, lax.rem(target, 32)

        def count(s, rank):
            same = targets[s // 4, lax.rem(s, 4)] // 32 == owner
            return rank + jnp.where(same, 1, 0)

        rank = lax.fori_loop(0, t, count, jnp.int32(0))
        source = jnp.where(lane == owner * CAP + rank, t, source)
        label = jnp.where((owner16 == owner) & (lane16 == slot), col * CAP + rank + 1, label)
        return source, label

    source, label = lax.fori_loop(
        0, 32, place, (jnp.zeros((8, 128), jnp.int32), jnp.zeros((16, 8, 128), jnp.int32))
    )
    label_out[...] = label
    for d in range(1, 16):
        peer = lax.rem(col + d, 16)
        send(label_out.at[peer], label_in.at[col], recv_l.at[d], (row, peer))
    table[0] = source
    copy = pltpu.make_async_copy(table.at[0], table_s.at[0], local_sem.at[0])
    copy.start()
    copy.wait()
    label_in[col] = label_out[col]

    half = PIECES // 2
    for dv in (0, 1):
        for p in range(PIECES):
            got_a(1, dv, p)
            if p < half:
                send_a(1, dv, p, "right")
            got_a(3, dv, p)
            if p >= half:
                send_a(3, dv, p, "left")
            got_b(1, dv, p)
            if p < half:
                send_b(1, dv, p, "right")
            got_b(3, dv, p)
            if p >= half:
                send_b(3, dv, p, "left")
            if dv == 0:
                got_a(0, 1, p)
                send_a(0, 1, p, "left")
                send_a(0, 1, p, "right")
                got_b(0, 1, p)
                send_b(0, 1, p, "left")
                send_b(0, 1, p, "right")
                send_a(0, 1, p, "core")
            send_a(1, dv, p, "core")
            send_a(3, dv, p, "core")

    odd = lax.rem(x + y, 2)
    first = lax.rem(x + 1 - odd, 4)
    second = lax.rem((1 - odd) * (x + 3) + odd * y, 4)
    third = lax.rem(x + 2, 4)
    fourth = lax.rem((1 - odd) * x + odd * (y + 2), 4)

    size = T // PARTS

    def dots(u, part):
        result = None
        for v in range(2):
            for c in range(2):
                left = a_all[u * 4 + v * 2 + c, :, pl.ds(part * size, size), :].reshape(8 * size, 4 * T)
                right = b_all[u * 2 + v, pl.ds(c * 4, 4)].reshape(4 * T, 4 * T)
                term = jnp.dot(left, right, preferred_element_type=jnp.float32)
                result = term if result is None else result + term
        return result

    for dv in (0, 1):
        for dx in (0, 1, 3):
            for p in range(PIECES):
                got_s(dx, dv, p)

    for dv in (0, 1):
        for p in range(PIECES):
            got_a(2, dv, p)
            send_a(2, dv, p, "core")
            got_b(2, dv, p)

    for d in range(1, 16):
        peer = lax.rem(col - d + 16, 16)
        landed(label_in.at[peer], recv_l.at[d], (row, peer))
    table[1] = jnp.sum(label_in[...], axis=0) - 1
    copy = pltpu.make_async_copy(table.at[1], table_s.at[1], local_sem.at[1])
    copy.start()
    copy.wait()

    for dv in (0, 1):
        for p in range(PIECES):
            got_s(2, dv, p)

    for part in range(PARTS):
        total[part] = dots(first, part)
        total[part] += dots(second, part)
        total[part] += dots(third, part)
        ladder = (total[part] + dots(fourth, part)).astype(jnp.bfloat16)
        ladder = ladder.reshape(8, size, 4 * T)
        for i in range(8):
            for j in range(4):
                tiles[part, i * 4 + j] = ladder[i, :, j * T:(j + 1) * T]

        def pack(k, carry):
            packed_parts[part][k] = tiles[part, jnp.clip(table_s[0, 0, k], 0, 31)]
            return carry

        lax.fori_loop(0, 16 * CAP, pack, 0)
        for d in range(1, 16):
            peer = lax.rem(col + d, 16)
            send(
                packed_parts[part].at[pl.ds(peer * CAP, CAP)], arrived_parts[part].at[pl.ds(col * CAP, CAP)],
                recv_d.at[part, d], (row, peer),
            )
        for k in range(CAP):
            arrived_parts[part][col * CAP + k] = packed_parts[part][col * CAP + k]

    for part in range(PARTS):
        for d in range(1, 16):
            peer = lax.rem(col - d + 16, 16)
            landed(arrived_parts[part].at[pl.ds(peer * CAP, CAP)], recv_d.at[part, d], (row, peer))

        def unpack(k, carry):
            out_ref[0, k, pl.ds(part * size, size), :] = arrived_parts[part][jnp.clip(table_s[1, 0, k], 0, 16 * CAP - 1)]
            return carry

        lax.fori_loop(0, 32, unpack, 0)
    for copy in started:
        copy.wait_send()


def on_device(integrals, amplitudes, integral_tiles, amplitude_tiles, targets):
    bf16 = jnp.bfloat16
    size = T // PARTS
    vmem, smem = pl.BlockSpec(memory_space=pltpu.VMEM), pl.BlockSpec(memory_space=pltpu.SMEM)
    dma = pltpu.SemaphoreType.DMA
    return pl.pallas_call(
        kernel,
        out_shape=jax.ShapeDtypeStruct((1, 32, T, T), bf16),
        in_specs=[vmem, vmem, smem, smem, smem],
        out_specs=vmem,
        scratch_shapes=[
            pltpu.VMEM((16, 8, T, 4 * T), bf16),
            pltpu.VMEM((8, 8, T, 4 * T), bf16),
            pltpu.VMEM((PARTS, 8 * size, 4 * T), jnp.float32),
            pltpu.VMEM((PARTS, 32, size, T), bf16),
            [pltpu.VMEM((16 * CAP, size, T), bf16) for _ in range(PARTS)],
            [pltpu.VMEM((16 * CAP, size, T), bf16) for _ in range(PARTS)],
            pltpu.VMEM((16, 8, 128), jnp.int32),
            pltpu.VMEM((16, 8, 128), jnp.int32),
            pltpu.VMEM((2, 8, 128), jnp.int32),
            pltpu.SMEM((2, 8, 128), jnp.int32),
            dma((256,)),
            dma((4, 2, PIECES)),
            dma((4, 2, PIECES)),
            dma((4, 2, PIECES)),
            dma((16,)),
            dma((PARTS, 16)),
            dma((2,)),
        ],
        compiler_params=pltpu.CompilerParams(
            collective_id=0, has_side_effects=True, vmem_limit_bytes=56 * 2**20
        ),
        cost_estimate=pl.CostEstimate(
            flops=2 * 1024 * 512 * 8192, bytes_accessed=3 * 2**20, transcendentals=0
        ),
    )(integrals, amplitudes, integral_tiles, amplitude_tiles, targets)


def solution(mesh):
    spec = P("row", "col")
    return jax.shard_map(
        on_device, mesh=mesh, in_specs=(spec,) * 5, out_specs=P("row", "col", None, None), check_vma=False
    )
```

```python
import functools

import jax
import jax.numpy as jnp
from jax import lax
from jax.experimental import pallas as pl
from jax.experimental.pallas import tpu as pltpu
from jax.sharding import PartitionSpec as P

MESH = pl.DeviceIdType.MESH
T = 128
CAP = 3
PIECES = 4
LATE = 0
GREET_ALL = False
SPREAD = [1, 15, 2, 14, 3, 13, 4, 12, 5, 11, 6, 10, 7, 9, 8]
PARTS = 2


class Sems:
    def __init__(self, ref):
        self.ref, self.used = ref, 0

    def take(self):
        self.used += 1
        return self.ref.at[self.used - 1]


def forwards(steps, dv, p):
    kept = (p < PIECES // 2) != (dv == 1 and PIECES - LATE == p)
    return steps == 1 and kept or steps == 3 and not kept


def arrival_order():
    queues = {(m, way): [] for m in "ab" for way in ("left", "right", "z")}
    left_over, order, now = {key: 0.0 for key in queues}, [], 0.0
    for m in "ab":
        for p in own_order():
            queues[m, "left"].append((3, 0, p))
            queues[m, "right"].append((1, 0, p))
        for p in own_order():
            if p < PIECES - LATE:
                queues[m, "z"].append((0, 1, p))
        for p in range(PIECES - LATE, PIECES):
            queues[m, "z"].append((0, 1, p))
    while any(queues.values()):
        both = queues["a", "z"] and queues["b", "z"]
        for (m, way), queue in queues.items():
            if queue:
                left_over[m, way] += 0.0625 if way == "z" and both else 0.125
        for (m, way), queue in queues.items():
            if queue and left_over[m, way] >= 1.0:
                left_over[m, way] = 0.0
                steps, dv, p = queue.pop(0)
                order.append((m, steps, dv, p))
                for how in onward(steps, dv, p):
                    if how == "z":
                        queues[m, "z"].append((steps, 1 - dv, p))
                    elif how == "right":
                        queues[m, "right"].append((steps + 1, dv, p))
                    else:
                        queues[m, "left"].append(((steps + 3) % 4, dv, p))
    return order


def own_order():
    return [*range(PIECES - LATE, PIECES), *range(PIECES - LATE)]


def onward(steps, dv, p):
    late = p >= PIECES - LATE
    ways = []
    if steps == 0 and dv == 1 and not late:
        ways += ["left", "right"]
    if steps in (1, 3) and not (dv == 1 and late) and forwards(steps, dv, p):
        ways.append("right" if steps == 1 else "left")
    if dv == 0 and late and steps:
        ways.append("z")
    return ways


def kernel(
    a_hbm, b_hbm, a_tiles, b_tiles, targets, arrived, slots_ref,
    a_in, b_in, a_all, b_all, total, tiles, packed_parts, label_out, label_in, table, table_s,
    send_ref, recv_a, recv_s, recv_b, recv_l, recv_d, local_sem,
):
    row, col = lax.axis_index("row"), lax.axis_index("col")
    y, zh = row // 2, row % 2
    x, zl, core = col // 4, (col // 2) % 2, col % 2
    sends = Sems(send_ref)
    started = []

    def col_of(dx, dv, dc):
        return lax.rem(x + dx + 4, 4) * 4 + lax.rem(zl + dv, 2) * 2 + lax.rem(core + dc, 2)

    def row_of(dy, dv):
        return lax.rem(y + dy + 4, 4) * 2 + lax.rem(zh + dv, 2)

    def send(src, dst, recv_sem, device):
        copy = pltpu.make_async_remote_copy(
            src_ref=src, dst_ref=dst, send_sem=sends.take(), recv_sem=recv_sem,
            device_id=device, device_id_type=MESH,
        )
        copy.start()
        started.append(copy)

    def landed(dst, recv_sem, device):
        pltpu.make_async_remote_copy(
            src_ref=dst, dst_ref=dst, send_sem=send_ref.at[0], recv_sem=recv_sem,
            device_id=device, device_id_type=MESH,
        ).wait_recv()

    barrier = pltpu.get_barrier_semaphore()
    if GREET_ALL:
        peers = [(row, lax.rem(col + d, 16)) for d in range(1, 16)]
    else:
        peers = [(row, col_of(1, 0, 0)), (row, col_of(-1, 0, 0)), (row, col_of(0, 1, 0)), (row, col_of(0, 0, 1))]
    peers += [(row_of(1, 0), col), (row_of(-1, 0), col), (row_of(0, 1), col)]
    for peer in peers:
        pl.semaphore_signal(barrier, inc=1, device_id=peer, device_id_type=MESH)

    rows_p = 8 // PIECES
    order = own_order()
    loads = []
    for n, p in enumerate(order):
        rows = pl.ds(p * rows_p * T, rows_p * T)
        loads.append((
            pltpu.make_async_copy(a_hbm.at[rows], a_in.at[rows], local_sem.at[2 + 2 * n]),
            pltpu.make_async_copy(b_hbm.at[rows], b_in.at[rows], local_sem.at[3 + 2 * n]),
        ))
        for load in loads[-1]:
            load.start()

    def mask(src, tile_flags, dst, p):
        for i in range(p * rows_p, (p + 1) * rows_p):
            for j in range(4):
                flag = tile_flags[j, i].astype(jnp.float32)
                block = src[pl.ds(i * T, T), pl.ds(j * T, T)].astype(jnp.float32) * flag
                dst[i, :, pl.ds(j * T, T)] = block.astype(jnp.bfloat16)

    def a_piece(dx, dv, dc, p):
        return a_all.at[col_of(-dx, dv, dc), pl.ds(p * rows_p, rows_p)]

    def b_piece(dy, dv, p):
        return b_all.at[row_of(-dy, dv), pl.ds(p * rows_p, rows_p)]

    def send_a(dx, dv, p, how):
        piece = a_piece(dx, dv, 0, p)
        if how == "right":
            send(piece, piece, recv_a.at[dx + 1, dv, p], (row, col_of(1, 0, 0)))
        elif how == "left":
            send(piece, piece, recv_a.at[(dx + 3) % 4, dv, p], (row, col_of(-1, 0, 0)))
        elif how == "z":
            send(piece, piece, recv_a.at[dx, 1 - dv, p], (row, col_of(0, 1, 0)))
        else:
            send(piece, piece, recv_s.at[dx, dv, p], (row, col_of(0, 0, 1)))

    def send_b(dy, dv, p, how):
        piece = b_piece(dy, dv, p)
        if how == "right":
            send(piece, piece, recv_b.at[dy + 1, dv, p], (row_of(1, 0), col))
        elif how == "left":
            send(piece, piece, recv_b.at[(dy + 3) % 4, dv, p], (row_of(-1, 0), col))
        else:
            send(piece, piece, recv_b.at[dy, 1 - dv, p], (row_of(0, 1), col))

    def got_s(dx, dv, p):
        landed(a_piece(dx, dv, 1, p), recv_s.at[dx, dv, p], (row, col_of(0, 0, 1)))

    mine_a, mine_b = a_all.at[col], b_all.at[row]
    for n, p in enumerate(order):
        late = p >= PIECES - LATE
        for load in loads[n]:
            load.wait()
        mask(a_in, a_tiles, mine_a, p)
        mask(b_in, b_tiles, mine_b, p)
        if n == 0:
            pl.semaphore_wait(barrier, len(peers))
        for one in (send_a, send_b):
            if not late:
                one(0, 0, p, "z")
            one(0, 0, p, "left")
            one(0, 0, p, "right")
    for p in range(PIECES - LATE, PIECES):
        send_a(0, 0, p, "z")
        send_b(0, 0, p, "z")
    for p in order:
        send_a(0, 0, p, "core")

    at_tile = lax.broadcasted_iota(jnp.int32, (32, 128), 0)
    lane = lax.broadcasted_iota(jnp.int32, (32, 128), 1)
    target = jnp.zeros((32, 128), jnp.int32)
    for t in range(32):
        target = jnp.where(at_tile == t, targets[t % 4, t // 4], target)
    owner, slot = target // 32, target % 32
    rank = jnp.zeros((32, 128), jnp.int32)
    for t in range(32):
        rank += jnp.where((at_tile > t) & (owner == targets[t % 4, t // 4] // 32), 1, 0)
    place = owner * CAP + rank
    table[0] = jnp.broadcast_to(
        jnp.sum(jnp.where(place == lane, at_tile, 0), axis=0, keepdims=True), (8, 128)
    )
    for w in range(16):
        here = jnp.where((owner == w) & (slot == lane), col * CAP + rank + 1, 0)
        label_out[w] = jnp.broadcast_to(jnp.sum(here, axis=0, keepdims=True), (8, 128))
    copy = pltpu.make_async_copy(table.at[0], table_s, local_sem.at[0])
    copy.start()
    copy.wait()

    odd = lax.rem(x + y, 2)
    near, far = lax.rem(x + 1, 4), lax.rem(x + 3, 4)
    size = T // PARTS

    def dots(quarter, v, part):
        result = None
        for c in range(2):
            left = a_all[quarter * 4 + v * 2 + c, :, pl.ds(part * size, size), :].reshape(8 * size, 4 * T)
            right = b_all[quarter * 2 + v, pl.ds(c * 4, 4)].reshape(4 * T, 4 * T)
            term = jnp.dot(left, right, preferred_element_type=jnp.float32)
            result = term if result is None else result + term
        return result

    def add_dots(opposite, part):
        def quarters(one, other):
            result = total[part] if opposite else None
            for quarter in (one, other):
                for v in range(2):
                    term = dots(quarter, v, part)
                    result = term if result is None else result + term
            total[part] = result

        @pl.when(odd == 0)
        def _():
            quarters(*((x, lax.rem(x + 2, 4)) if opposite else (near, far)))

        @pl.when(odd == 1)
        def _():
            quarters(*((lax.rem(x + 2, 4), lax.rem(y + 2, 4)) if opposite else (x, y)))

    todo = {(m, steps, dv, p) for m in "abs" for steps in range(4) for dv in range(2) for p in range(PIECES)}
    todo -= {("a", 0, 0, p) for p in range(PIECES)} | {("b", 0, 0, p) for p in range(PIECES)}

    def need(steps, dv):
        for p in range(PIECES):
            if ("s", steps, dv, p) in todo:
                todo.discard(("s", steps, dv, p))
                got_s(steps, dv, p)

    early = False
    for m, steps, dv, p in arrival_order():
        todo.discard((m, steps, dv, p))
        if m == "a":
            landed(a_piece(steps, dv, 0, p), recv_a.at[steps, dv, p], (row, col_of(0, 1, 0)))
        else:
            landed(b_piece(steps, dv, p), recv_b.at[steps, dv, p], (row_of(0, 1), col))
        for how in onward(steps, dv, p):
            (send_a if m == "a" else send_b)(steps, dv, p, how)
        if m == "a":
            send_a(steps, dv, p, "core")
        if not early and not any(n != "s" and d != 2 for n, d, _, _ in todo):
            early = True
            for d in range(1, 16):
                peer = lax.rem(col + d, 16)
                send(label_out.at[peer], label_in.at[col], recv_l.at[d], (row, peer))
            label_in[col] = label_out[col]
            for dx in (0, 1, 3):
                for dv in range(2):
                    need(dx, dv)
            for part in range(PARTS):
                add_dots(False, part)

    for d in range(1, 16):
        peer = lax.rem(col - d + 16, 16)
        landed(label_in.at[peer], recv_l.at[d], (row, peer))
    slots_ref[...] = jnp.clip(jnp.sum(label_in[...], axis=0) - 1, 0, 16 * CAP - 1)

    for dv in range(2):
        need(2, dv)

    stays = []
    for part in range(PARTS):
        add_dots(True, part)
        ladder = total[part].astype(jnp.bfloat16).reshape(8, size, 4 * T)
        for i in range(8):
            for j in range(4):
                tiles[part, i * 4 + j] = ladder[i, :, j * T:(j + 1) * T]

        def pack(k, carry):
            packed_parts[part][k] = tiles[part, jnp.clip(table_s[0, k], 0, 31)]
            return carry

        lax.fori_loop(0, 16 * CAP, pack, 0, unroll=4)
        rows = pl.ds(part * size, size)
        for d in SPREAD:
            peer = lax.rem(col + d, 16)
            send(
                packed_parts[part].at[pl.ds(peer * CAP, CAP)], arrived.at[pl.ds(col * CAP, CAP), rows],
                recv_d.at[part, d], (row, peer),
            )
        stays.append(pltpu.make_async_copy(
            packed_parts[part].at[pl.ds(col * CAP, CAP)], arrived.at[pl.ds(col * CAP, CAP), rows],
            local_sem.at[2 + part],
        ))
        stays[-1].start()

    for part in range(PARTS):
        rows = pl.ds(part * size, size)
        stays[part].wait()
        for d in SPREAD:
            peer = lax.rem(col - d + 16, 16)
            landed(arrived.at[pl.ds(peer * CAP, CAP), rows], recv_d.at[part, d], (row, peer))
    for copy in started:
        copy.wait_send()


def unpack(slots, arrived, owned):
    def one(k, carry):
        owned[0, k] = arrived[slots[0, k]]
        return carry

    lax.fori_loop(0, 32, one, 0, unroll=4)


def on_device(integrals, amplitudes, integral_tiles, amplitude_tiles, targets):
    bf16 = jnp.bfloat16
    size = T // PARTS
    vmem, smem, hbm = (pl.BlockSpec(memory_space=s) for s in (pltpu.VMEM, pltpu.SMEM, pl.ANY))
    dma = pltpu.SemaphoreType.DMA
    arrived, slots = pl.pallas_call(
        kernel,
        out_shape=(
            jax.ShapeDtypeStruct((16 * CAP, T, T), bf16),
            jax.ShapeDtypeStruct((8, 128), jnp.int32),
        ),
        in_specs=[hbm, hbm, smem, smem, smem],
        out_specs=(hbm, vmem),
        scratch_shapes=[
            pltpu.VMEM((8 * T, 4 * T), bf16),
            pltpu.VMEM((8 * T, 4 * T), bf16),
            pltpu.VMEM((16, 8, T, 4 * T), bf16),
            pltpu.VMEM((8, 8, T, 4 * T), bf16),
            pltpu.VMEM((PARTS, 8 * size, 4 * T), jnp.float32),
            pltpu.VMEM((PARTS, 32, size, T), bf16),
            [pltpu.VMEM((16 * CAP, size, T), bf16) for _ in range(PARTS)],
            pltpu.VMEM((16, 8, 128), jnp.int32),
            pltpu.VMEM((16, 8, 128), jnp.int32),
            pltpu.VMEM((1, 8, 128), jnp.int32),
            pltpu.SMEM((8, 128), jnp.int32),
            dma((320,)),
            dma((4, 2, PIECES)),
            dma((4, 2, PIECES)),
            dma((4, 2, PIECES)),
            dma((16,)),
            dma((PARTS, 16)),
            dma((2 + 2 * PIECES,)),
        ],
        compiler_params=pltpu.CompilerParams(
            collective_id=0, has_side_effects=True, vmem_limit_bytes=56 * 2**20
        ),
        cost_estimate=pl.CostEstimate(
            flops=2 * 1024 * 512 * 8192, bytes_accessed=4 * 2**20, transcendentals=0
        ),
    )(integrals, amplitudes, integral_tiles.T, amplitude_tiles.T, targets.T)
    return pl.pallas_call(
        unpack,
        out_shape=jax.ShapeDtypeStruct((1, 32, T, T), bf16),
        in_specs=[smem, vmem],
        out_specs=vmem,
    )(slots, arrived)


def solution(mesh):
    spec = P("row", "col")
    return jax.shard_map(
        on_device, mesh=mesh, in_specs=(spec,) * 5, out_specs=P("row", "col", None, None), check_vma=False
    )
```

```python
import functools

import jax
import jax.numpy as jnp
from jax import lax
from jax.experimental import pallas as pl
from jax.experimental.pallas import tpu as pltpu
from jax.sharding import PartitionSpec as P

MESH = pl.DeviceIdType.MESH
T = 128
CAP = 3
PIECES = 8
LATE = 1
GREET_ALL = False
SPREAD = [1, 15, 2, 14, 3, 13, 4, 12, 5, 11, 6, 10, 7, 9, 8]
PARTS = 2


class Sems:
    def __init__(self, ref):
        self.ref, self.used = ref, 0

    def take(self):
        self.used += 1
        return self.ref.at[self.used - 1]


def forwards(steps, dv, p):
    kept = (p < PIECES // 2) != (dv == 1 and PIECES - LATE == p)
    return steps == 1 and kept or steps == 3 and not kept


def arrival_order():
    queues = {(m, way): [] for m in "ab" for way in ("left", "right", "z")}
    left_over, order, now = {key: 0.0 for key in queues}, [], 0.0
    for m in "ab":
        for p in own_order():
            queues[m, "left"].append((3, 0, p))
            queues[m, "right"].append((1, 0, p))
        for p in own_order():
            if p < PIECES - LATE:
                queues[m, "z"].append((0, 1, p))
        for p in range(PIECES - LATE, PIECES):
            queues[m, "z"].append((0, 1, p))
    while any(queues.values()):
        both = queues["a", "z"] and queues["b", "z"]
        for (m, way), queue in queues.items():
            if queue:
                left_over[m, way] += 0.0625 if way == "z" and both else 0.125
        for (m, way), queue in queues.items():
            if queue and left_over[m, way] >= 1.0:
                left_over[m, way] = 0.0
                steps, dv, p = queue.pop(0)
                order.append((m, steps, dv, p))
                for how in onward(steps, dv, p):
                    if how == "z":
                        queues[m, "z"].append((steps, 1 - dv, p))
                    elif how == "right":
                        queues[m, "right"].append((steps + 1, dv, p))
                    else:
                        queues[m, "left"].append(((steps + 3) % 4, dv, p))
    return order


def own_order():
    return [*range(PIECES - LATE, PIECES), *range(PIECES - LATE)]


def onward(steps, dv, p):
    late = p >= PIECES - LATE
    ways = []
    if steps == 0 and dv == 1 and not late:
        ways += ["left", "right"]
    if steps in (1, 3) and not (dv == 1 and late) and forwards(steps, dv, p):
        ways.append("right" if steps == 1 else "left")
    if dv == 0 and late and steps:
        ways.append("z")
    return ways


def kernel(
    a_hbm, b_hbm, a_tiles, b_tiles, targets, arrived, slots_ref,
    a_in, b_in, a_all, b_all, total, tiles, packed_parts, label_out, label_in, table, table_s,
    send_ref, recv_a, recv_s, recv_b, recv_l, recv_d, local_sem,
):
    row, col = lax.axis_index("row"), lax.axis_index("col")
    y, zh = row // 2, row % 2
    x, zl, core = col // 4, (col // 2) % 2, col % 2
    sends = Sems(send_ref)
    started = []

    def col_of(dx, dv, dc):
        return lax.rem(x + dx + 4, 4) * 4 + lax.rem(zl + dv, 2) * 2 + lax.rem(core + dc, 2)

    def row_of(dy, dv):
        return lax.rem(y + dy + 4, 4) * 2 + lax.rem(zh + dv, 2)

    def send(src, dst, recv_sem, device):
        copy = pltpu.make_async_remote_copy(
            src_ref=src, dst_ref=dst, send_sem=sends.take(), recv_sem=recv_sem,
            device_id=device, device_id_type=MESH,
        )
        copy.start()
        started.append(copy)

    def landed(dst, recv_sem, device):
        pltpu.make_async_remote_copy(
            src_ref=dst, dst_ref=dst, send_sem=send_ref.at[0], recv_sem=recv_sem,
            device_id=device, device_id_type=MESH,
        ).wait_recv()

    barrier = pltpu.get_barrier_semaphore()
    if GREET_ALL:
        peers = [(row, lax.rem(col + d, 16)) for d in range(1, 16)]
    else:
        peers = [(row, col_of(1, 0, 0)), (row, col_of(-1, 0, 0)), (row, col_of(0, 1, 0)), (row, col_of(0, 0, 1))]
    peers += [(row_of(1, 0), col), (row_of(-1, 0), col), (row_of(0, 1), col)]
    for peer in peers:
        pl.semaphore_signal(barrier, inc=1, device_id=peer, device_id_type=MESH)

    rows_p = 8 // PIECES
    order = own_order()
    loads = []
    for n, p in enumerate(order):
        rows = pl.ds(p * rows_p * T, rows_p * T)
        loads.append((
            pltpu.make_async_copy(a_hbm.at[rows], a_in.at[rows], local_sem.at[2 + 2 * n]),
            pltpu.make_async_copy(b_hbm.at[rows], b_in.at[rows], local_sem.at[3 + 2 * n]),
        ))
        for load in loads[-1]:
            load.start()

    def mask(src, tile_flags, dst, p):
        for i in range(p * rows_p, (p + 1) * rows_p):
            for j in range(4):
                flag = tile_flags[j, i].astype(jnp.float32)
                block = src[pl.ds(i * T, T), pl.ds(j * T, T)].astype(jnp.float32) * flag
                dst[i, :, pl.ds(j * T, T)] = block.astype(jnp.bfloat16)

    def a_piece(dx, dv, dc, p):
        return a_all.at[col_of(-dx, dv, dc), pl.ds(p * rows_p, rows_p)]

    def b_piece(dy, dv, p):
        return b_all.at[row_of(-dy, dv), pl.ds(p * rows_p, rows_p)]

    def send_a(dx, dv, p, how):
        piece = a_piece(dx, dv, 0, p)
        if how == "right":
            send(piece, piece, recv_a.at[dx + 1, dv, p], (row, col_of(1, 0, 0)))
        elif how == "left":
            send(piece, piece, recv_a.at[(dx + 3) % 4, dv, p], (row, col_of(-1, 0, 0)))
        elif how == "z":
            send(piece, piece, recv_a.at[dx, 1 - dv, p], (row, col_of(0, 1, 0)))
        else:
            send(piece, piece, recv_s.at[dx, dv, p], (row, col_of(0, 0, 1)))

    def send_b(dy, dv, p, how):
        piece = b_piece(dy, dv, p)
        if how == "right":
            send(piece, piece, recv_b.at[dy + 1, dv, p], (row_of(1, 0), col))
        elif how == "left":
            send(piece, piece, recv_b.at[(dy + 3) % 4, dv, p], (row_of(-1, 0), col))
        else:
            send(piece, piece, recv_b.at[dy, 1 - dv, p], (row_of(0, 1), col))

    def got_s(dx, dv, p):
        landed(a_piece(dx, dv, 1, p), recv_s.at[dx, dv, p], (row, col_of(0, 0, 1)))

    mine_a, mine_b = a_all.at[col], b_all.at[row]
    for n, p in enumerate(order):
        late = p >= PIECES - LATE
        for load in loads[n]:
            load.wait()
        mask(a_in, a_tiles, mine_a, p)
        mask(b_in, b_tiles, mine_b, p)
        if n == 0:
            pl.semaphore_wait(barrier, len(peers))
        for one in (send_a, send_b):
            if not late:
                one(0, 0, p, "z")
            one(0, 0, p, "left")
            one(0, 0, p, "right")
    for p in range(PIECES - LATE, PIECES):
        send_a(0, 0, p, "z")
        send_b(0, 0, p, "z")
    for p in order:
        send_a(0, 0, p, "core")

    at_tile = lax.broadcasted_iota(jnp.int32, (32, 128), 0)
    lane = lax.broadcasted_iota(jnp.int32, (32, 128), 1)
    target = jnp.zeros((32, 128), jnp.int32)
    for t in range(32):
        target = jnp.where(at_tile == t, targets[t % 4, t // 4], target)
    owner, slot = target // 32, target % 32
    rank = jnp.zeros((32, 128), jnp.int32)
    for t in range(32):
        rank += jnp.where((at_tile > t) & (owner == targets[t % 4, t // 4] // 32), 1, 0)
    place = owner * CAP + rank
    table[0] = jnp.broadcast_to(
        jnp.sum(jnp.where(place == lane, at_tile, 0), axis=0, keepdims=True), (8, 128)
    )
    for w in range(16):
        here = jnp.where((owner == w) & (slot == lane), col * CAP + rank + 1, 0)
        label_out[w] = jnp.broadcast_to(jnp.sum(here, axis=0, keepdims=True), (8, 128))
    copy = pltpu.make_async_copy(table.at[0], table_s, local_sem.at[0])
    copy.start()
    copy.wait()

    odd = lax.rem(x + y, 2)
    near, far = lax.rem(x + 1, 4), lax.rem(x + 3, 4)
    size = T // PARTS

    def dots(quarter, v, part):
        result = None
        for c in range(2):
            left = a_all[quarter * 4 + v * 2 + c, :, pl.ds(part * size, size), :].reshape(8 * size, 4 * T)
            right = b_all[quarter * 2 + v, pl.ds(c * 4, 4)].reshape(4 * T, 4 * T)
            term = jnp.dot(left, right, preferred_element_type=jnp.float32)
            result = term if result is None else result + term
        return result

    def add_dots(opposite, part):
        def quarters(one, other):
            result = total[part] if opposite else None
            for quarter in (one, other):
                for v in range(2):
                    term = dots(quarter, v, part)
                    result = term if result is None else result + term
            total[part] = result

        @pl.when(odd == 0)
        def _():
            quarters(*((x, lax.rem(x + 2, 4)) if opposite else (near, far)))

        @pl.when(odd == 1)
        def _():
            quarters(*((lax.rem(x + 2, 4), lax.rem(y + 2, 4)) if opposite else (x, y)))

    todo = {(m, steps, dv, p) for m in "abs" for steps in range(4) for dv in range(2) for p in range(PIECES)}
    todo -= {("a", 0, 0, p) for p in range(PIECES)} | {("b", 0, 0, p) for p in range(PIECES)}

    def need(steps, dv):
        for p in range(PIECES):
            if ("s", steps, dv, p) in todo:
                todo.discard(("s", steps, dv, p))
                got_s(steps, dv, p)

    early = False
    for m, steps, dv, p in arrival_order():
        todo.discard((m, steps, dv, p))
        if m == "a":
            landed(a_piece(steps, dv, 0, p), recv_a.at[steps, dv, p], (row, col_of(0, 1, 0)))
        else:
            landed(b_piece(steps, dv, p), recv_b.at[steps, dv, p], (row_of(0, 1), col))
        for how in onward(steps, dv, p):
            (send_a if m == "a" else send_b)(steps, dv, p, how)
        if m == "a":
            send_a(steps, dv, p, "core")
        if not early and not any(n != "s" and d != 2 for n, d, _, _ in todo):
            early = True
            for d in range(1, 16):
                peer = lax.rem(col + d, 16)
                send(label_out.at[peer], label_in.at[col], recv_l.at[d], (row, peer))
            label_in[col] = label_out[col]
            for dx in (0, 1, 3):
                for dv in range(2):
                    need(dx, dv)
            for part in range(PARTS):
                add_dots(False, part)

    for d in range(1, 16):
        peer = lax.rem(col - d + 16, 16)
        landed(label_in.at[peer], recv_l.at[d], (row, peer))
    slots_ref[...] = jnp.clip(jnp.sum(label_in[...], axis=0) - 1, 0, 16 * CAP - 1)

    for dv in range(2):
        need(2, dv)

    stays = []
    for part in range(PARTS):
        add_dots(True, part)
        ladder = total[part].astype(jnp.bfloat16).reshape(8, size, 4 * T)
        for i in range(8):
            for j in range(4):
                tiles[part, i * 4 + j] = ladder[i, :, j * T:(j + 1) * T]

        def pack(k, carry):
            packed_parts[part][k] = tiles[part, jnp.clip(table_s[0, k], 0, 31)]
            return carry

        lax.fori_loop(0, 16 * CAP, pack, 0, unroll=4)
        rows = pl.ds(part * size, size)
        for d in SPREAD:
            peer = lax.rem(col + d, 16)
            send(
                packed_parts[part].at[pl.ds(peer * CAP, CAP)], arrived.at[pl.ds(col * CAP, CAP), rows],
                recv_d.at[part, d], (row, peer),
            )
        stays.append(pltpu.make_async_copy(
            packed_parts[part].at[pl.ds(col * CAP, CAP)], arrived.at[pl.ds(col * CAP, CAP), rows],
            local_sem.at[2 + part],
        ))
        stays[-1].start()

    for part in range(PARTS):
        rows = pl.ds(part * size, size)
        stays[part].wait()
        for d in SPREAD:
            peer = lax.rem(col - d + 16, 16)
            landed(arrived.at[pl.ds(peer * CAP, CAP), rows], recv_d.at[part, d], (row, peer))
    for copy in started:
        copy.wait_send()


def unpack(slots, arrived, owned):
    def one(k, carry):
        owned[0, k] = arrived[slots[0, k]]
        return carry

    lax.fori_loop(0, 32, one, 0, unroll=4)


def on_device(integrals, amplitudes, integral_tiles, amplitude_tiles, targets):
    bf16 = jnp.bfloat16
    size = T // PARTS
    vmem, smem, hbm = (pl.BlockSpec(memory_space=s) for s in (pltpu.VMEM, pltpu.SMEM, pl.ANY))
    dma = pltpu.SemaphoreType.DMA
    arrived, slots = pl.pallas_call(
        kernel,
        out_shape=(
            jax.ShapeDtypeStruct((16 * CAP, T, T), bf16),
            jax.ShapeDtypeStruct((8, 128), jnp.int32),
        ),
        in_specs=[hbm, hbm, smem, smem, smem],
        out_specs=(hbm, vmem),
        scratch_shapes=[
            pltpu.VMEM((8 * T, 4 * T), bf16),
            pltpu.VMEM((8 * T, 4 * T), bf16),
            pltpu.VMEM((16, 8, T, 4 * T), bf16),
            pltpu.VMEM((8, 8, T, 4 * T), bf16),
            pltpu.VMEM((PARTS, 8 * size, 4 * T), jnp.float32),
            pltpu.VMEM((PARTS, 32, size, T), bf16),
            [pltpu.VMEM((16 * CAP, size, T), bf16) for _ in range(PARTS)],
            pltpu.VMEM((16, 8, 128), jnp.int32),
            pltpu.VMEM((16, 8, 128), jnp.int32),
            pltpu.VMEM((1, 8, 128), jnp.int32),
            pltpu.SMEM((8, 128), jnp.int32),
            dma((320,)),
            dma((4, 2, PIECES)),
            dma((4, 2, PIECES)),
            dma((4, 2, PIECES)),
            dma((16,)),
            dma((PARTS, 16)),
            dma((2 + 2 * PIECES,)),
        ],
        compiler_params=pltpu.CompilerParams(
            collective_id=0, has_side_effects=True, vmem_limit_bytes=56 * 2**20
        ),
        cost_estimate=pl.CostEstimate(
            flops=2 * 1024 * 512 * 8192, bytes_accessed=4 * 2**20, transcendentals=0
        ),
    )(integrals, amplitudes, integral_tiles.T, amplitude_tiles.T, targets.T)
    return pl.pallas_call(
        unpack,
        out_shape=jax.ShapeDtypeStruct((1, 32, T, T), bf16),
        in_specs=[smem, vmem],
        out_specs=vmem,
    )(slots, arrived)


def solution(mesh):
    spec = P("row", "col")
    return jax.shard_map(
        on_device, mesh=mesh, in_specs=(spec,) * 5, out_specs=P("row", "col", None, None), check_vma=False
    )
```

```python
import functools

import jax
import jax.numpy as jnp
from jax import lax
from jax.experimental import pallas as pl
from jax.experimental.pallas import tpu as pltpu
from jax.sharding import PartitionSpec as P

MESH = pl.DeviceIdType.MESH
T = 128
CAP = 3
PIECES = 8
LATE = 1
SPREAD = [1, 15, 2, 14, 3, 13, 4, 12, 5, 11, 6, 10, 7, 9, 8]
PARTS = ((0, 32), (32, 80), (80, 128))


class Sems:
    def __init__(self, ref):
        self.ref, self.used = ref, 0

    def take(self):
        self.used += 1
        return self.ref.at[self.used - 1]


def forwards(steps, dv, p):
    kept = (p < PIECES // 2) != (dv == 1 and PIECES - LATE == p)
    return steps == 1 and kept or steps == 3 and not kept


def arrival_order():
    queues = {(m, way): [] for m in "ab" for way in ("left", "right", "z")}
    left_over, order, now = {key: 0.0 for key in queues}, [], 0.0
    for m in "ab":
        for p in own_order():
            queues[m, "left"].append((3, 0, p))
            queues[m, "right"].append((1, 0, p))
        for p in own_order():
            if p < PIECES - LATE:
                queues[m, "z"].append((0, 1, p))
        for p in range(PIECES - LATE, PIECES):
            queues[m, "z"].append((0, 1, p))
    while any(queues.values()):
        both = queues["a", "z"] and queues["b", "z"]
        for (m, way), queue in queues.items():
            if queue:
                left_over[m, way] += 0.0625 if way == "z" and both else 0.125
        for (m, way), queue in queues.items():
            if queue and left_over[m, way] >= 1.0:
                left_over[m, way] = 0.0
                steps, dv, p = queue.pop(0)
                order.append((m, steps, dv, p))
                for how in onward(steps, dv, p):
                    if how == "z":
                        queues[m, "z"].append((steps, 1 - dv, p))
                    elif how == "right":
                        queues[m, "right"].append((steps + 1, dv, p))
                    else:
                        queues[m, "left"].append(((steps + 3) % 4, dv, p))
    return order


def own_order():
    return [*range(PIECES - LATE, PIECES), *range(PIECES - LATE)]


def onward(steps, dv, p):
    late = p >= PIECES - LATE
    ways = []
    if steps == 0 and dv == 1 and not late:
        ways += ["left", "right"]
    if steps in (1, 3) and not (dv == 1 and late) and forwards(steps, dv, p):
        ways.append("right" if steps == 1 else "left")
    if dv == 0 and late and steps:
        ways.append("z")
    return ways


def kernel(
    a_hbm, b_hbm, a_tiles, b_tiles, targets, arrived, slots_ref,
    a_in, b_in, a_all, b_all, total, tiles, packed_parts, label_out, label_in, table, table_s,
    send_ref, recv_a, recv_s, recv_b, recv_l, recv_d, local_sem,
):
    row, col = lax.axis_index("row"), lax.axis_index("col")
    y, zh = row // 2, row % 2
    x, zl, core = col // 4, (col // 2) % 2, col % 2
    sends = Sems(send_ref)
    started = []

    def col_of(dx, dv, dc):
        return lax.rem(x + dx + 4, 4) * 4 + lax.rem(zl + dv, 2) * 2 + lax.rem(core + dc, 2)

    def row_of(dy, dv):
        return lax.rem(y + dy + 4, 4) * 2 + lax.rem(zh + dv, 2)

    def send(src, dst, recv_sem, device):
        copy = pltpu.make_async_remote_copy(
            src_ref=src, dst_ref=dst, send_sem=sends.take(), recv_sem=recv_sem,
            device_id=device, device_id_type=MESH,
        )
        copy.start()
        started.append(copy)

    def landed(dst, recv_sem, device):
        pltpu.make_async_remote_copy(
            src_ref=dst, dst_ref=dst, send_sem=send_ref.at[0], recv_sem=recv_sem,
            device_id=device, device_id_type=MESH,
        ).wait_recv()

    barrier = pltpu.get_barrier_semaphore()
    peers = [(row, col_of(1, 0, 0)), (row, col_of(-1, 0, 0)), (row, col_of(0, 1, 0)), (row, col_of(0, 0, 1))]
    peers += [(row_of(1, 0), col), (row_of(-1, 0), col), (row_of(0, 1), col)]
    for peer in peers:
        pl.semaphore_signal(barrier, inc=1, device_id=peer, device_id_type=MESH)

    order = own_order()
    loads = []
    for n, p in enumerate(order):
        thin = pl.ds(p * 16, 16)
        loads.append((
            pltpu.make_async_copy(a_hbm.at[:, thin], a_in.at[:, thin], local_sem.at[2 + 2 * n]),
            pltpu.make_async_copy(b_hbm.at[p], b_in.at[p], local_sem.at[3 + 2 * n]),
        ))
        for load in loads[-1]:
            load.start()

    def mask(src, tile_flags, dst, i, rows):
        for j in range(4):
            flag = tile_flags[j, i].astype(jnp.float32)
            block = src[i, rows, pl.ds(j * T, T)].astype(jnp.float32) * flag
            dst[i, rows, pl.ds(j * T, T)] = block.astype(jnp.bfloat16)

    def a_piece(dx, dv, dc, p):
        return a_all.at[col_of(-dx, dv, dc), :, pl.ds(p * 16, 16)]

    def b_piece(dy, dv, p):
        return b_all.at[row_of(-dy, dv), p]

    def send_a(dx, dv, p, how):
        piece = a_piece(dx, dv, 0, p)
        if how == "right":
            send(piece, piece, recv_a.at[dx + 1, dv, p], (row, col_of(1, 0, 0)))
        elif how == "left":
            send(piece, piece, recv_a.at[(dx + 3) % 4, dv, p], (row, col_of(-1, 0, 0)))
        elif how == "z":
            send(piece, piece, recv_a.at[dx, 1 - dv, p], (row, col_of(0, 1, 0)))
        else:
            send(piece, piece, recv_s.at[dx, dv, p], (row, col_of(0, 0, 1)))

    def send_b(dy, dv, p, how):
        piece = b_piece(dy, dv, p)
        if how == "right":
            send(piece, piece, recv_b.at[dy + 1, dv, p], (row_of(1, 0), col))
        elif how == "left":
            send(piece, piece, recv_b.at[(dy + 3) % 4, dv, p], (row_of(-1, 0), col))
        else:
            send(piece, piece, recv_b.at[dy, 1 - dv, p], (row_of(0, 1), col))

    def got_s(dx, dv, p):
        landed(a_piece(dx, dv, 1, p), recv_s.at[dx, dv, p], (row, col_of(0, 0, 1)))

    mine_a, mine_b = a_all.at[col], b_all.at[row]
    for n, p in enumerate(order):
        late = p >= PIECES - LATE
        for load in loads[n]:
            load.wait()
        for i in range(8):
            mask(a_in, a_tiles, mine_a, i, pl.ds(p * 16, 16))
        mask(b_in, b_tiles, mine_b, p, pl.ds(0, T))
        if n == 0:
            pl.semaphore_wait(barrier, len(peers))
        for one in (send_a, send_b):
            if not late:
                one(0, 0, p, "z")
            one(0, 0, p, "left")
            one(0, 0, p, "right")
    for p in range(PIECES - LATE, PIECES):
        send_a(0, 0, p, "z")
        send_b(0, 0, p, "z")
    for p in order:
        send_a(0, 0, p, "core")

    at_tile = lax.broadcasted_iota(jnp.int32, (32, 128), 0)
    lane = lax.broadcasted_iota(jnp.int32, (32, 128), 1)
    target = jnp.zeros((32, 128), jnp.int32)
    for t in range(32):
        target = jnp.where(at_tile == t, targets[t % 4, t // 4], target)
    owner, slot = target // 32, target % 32
    rank = jnp.zeros((32, 128), jnp.int32)
    for t in range(32):
        rank += jnp.where((at_tile > t) & (owner == targets[t % 4, t // 4] // 32), 1, 0)
    place = owner * CAP + rank
    table[0] = jnp.broadcast_to(
        jnp.sum(jnp.where(place == lane, at_tile, 0), axis=0, keepdims=True), (8, 128)
    )
    for w in range(16):
        here = jnp.where((owner == w) & (slot == lane), col * CAP + rank + 1, 0)
        label_out[w] = jnp.broadcast_to(jnp.sum(here, axis=0, keepdims=True), (8, 128))
    copy = pltpu.make_async_copy(table.at[0], table_s, local_sem.at[0])
    copy.start()
    copy.wait()

    odd = lax.rem(x + y, 2)
    near, far = lax.rem(x + 1, 4), lax.rem(x + 3, 4)

    def dots(result, quarters, rows, k_tiles):
        count = rows[1] - rows[0]
        for quarter in quarters:
            for v in range(2):
                for c in range(2):
                    k = [t - 4 * c for t in k_tiles if t // 4 == c]
                    if not k:
                        continue
                    left = a_all[quarter * 4 + v * 2 + c, :, rows[0]:rows[1], k[0] * T:(k[-1] + 1) * T]
                    right = b_all[quarter * 2 + v, 4 * c + k[0]:4 * c + k[-1] + 1]
                    term = jnp.dot(
                        left.reshape(8 * count, len(k) * T), right.reshape(len(k) * T, 4 * T),
                        preferred_element_type=jnp.float32,
                    )
                    result = term if result is None else result + term
        return result

    early_quarters = ((near, far), (x, y))
    last_quarters = ((x, lax.rem(x + 2, 4)), (lax.rem(x + 2, 4), lax.rem(y + 2, 4)))

    def for_parity(step):
        for parity in range(2):
            @pl.when(odd == parity)
            def _():
                total[...] = step(early_quarters[parity], last_quarters[parity])

    todo = {(m, steps, dv, p) for m in "abs" for steps in range(4) for dv in range(2) for p in range(PIECES)}
    todo -= {(m, 0, 0, p) for p in range(PIECES) for m in "ab"}

    def of_part(part, steps):
        lo, hi = part
        return {("a", d, dv, p) for d in steps for dv in range(2) for p in range(lo // 16, hi // 16)}

    def need(part, steps):
        for _, d, dv, p in sorted(of_part(part, steps)):
            if ("s", d, dv, p) in todo:
                todo.discard(("s", d, dv, p))
                landed(a_piece(d, dv, 1, p), recv_s.at[d, dv, p], (row, col_of(0, 0, 1)))

    head, late_k = PARTS[0], range(PIECES - LATE, PIECES)
    early_k = range(PIECES - LATE)
    early_set = of_part(head, (0, 1, 3)) | {("b", d, dv, p) for d in (0, 1, 3) for dv in range(2) for p in early_k}
    early = False
    for m, steps, dv, p in arrival_order():
        todo.discard((m, steps, dv, p))
        if m == "a":
            landed(a_piece(steps, dv, 0, p), recv_a.at[steps, dv, p], (row, col_of(0, 1, 0)))
        else:
            landed(b_piece(steps, dv, p), recv_b.at[steps, dv, p], (row_of(0, 1), col))
        for how in onward(steps, dv, p):
            (send_a if m == "a" else send_b)(steps, dv, p, how)
        if m == "a":
            send_a(steps, dv, p, "core")
        if not early and not early_set & todo:
            early = True
            for d in range(1, 16):
                peer = lax.rem(col + d, 16)
                send(label_out.at[peer], label_in.at[col], recv_l.at[d], (row, peer))
            label_in[col] = label_out[col]
            need(head, (0, 1, 3))
            for_parity(lambda first, last: dots(None, first, head, early_k))

    for d in range(1, 16):
        peer = lax.rem(col - d + 16, 16)
        landed(label_in.at[peer], recv_l.at[d], (row, peer))
    slots_ref[...] = jnp.clip(jnp.sum(label_in[...], axis=0) - 1, 0, 16 * CAP - 1)

    stays = []
    for n, part in enumerate(PARTS):
        need(part, range(4))
        lo, hi = part
        if n == 0:
            for_parity(lambda first, last: dots(dots(total[...], first, part, late_k), last, part, range(8)))
            ladder = total[...]
        else:
            ladder = dots(None, range(4), part, range(8))
        ladder = ladder.astype(jnp.bfloat16).reshape(8, hi - lo, 4 * T)
        for i in range(8):
            for j in range(4):
                tiles[i * 4 + j, lo:hi] = ladder[i, :, j * T:(j + 1) * T]

        def pack(k, carry):
            packed_parts[n][k] = tiles[jnp.clip(table_s[0, k], 0, 31), lo:hi]
            return carry

        lax.fori_loop(0, 16 * CAP, pack, 0, unroll=4)
        rows = pl.ds(lo, hi - lo)
        for d in SPREAD:
            peer = lax.rem(col + d, 16)
            send(
                packed_parts[n].at[pl.ds(peer * CAP, CAP)], arrived.at[pl.ds(col * CAP, CAP), rows],
                recv_d.at[n, d], (row, peer),
            )
        stays.append(pltpu.make_async_copy(
            packed_parts[n].at[pl.ds(col * CAP, CAP)], arrived.at[pl.ds(col * CAP, CAP), rows],
            local_sem.at[2 + n],
        ))
        stays[-1].start()

    for n, (lo, hi) in enumerate(PARTS):
        rows = pl.ds(lo, hi - lo)
        stays[n].wait()
        for d in SPREAD:
            peer = lax.rem(col - d + 16, 16)
            landed(arrived.at[pl.ds(peer * CAP, CAP), rows], recv_d.at[n, d], (row, peer))
    for copy in started:
        copy.wait_send()


def unpack(slots, arrived, owned):
    def one(k, carry):
        owned[0, k] = arrived[slots[0, k]]
        return carry

    lax.fori_loop(0, 32, one, 0, unroll=4)


def on_device(integrals, amplitudes, integral_tiles, amplitude_tiles, targets):
    bf16 = jnp.bfloat16
    vmem, smem, hbm = (pl.BlockSpec(memory_space=s) for s in (pltpu.VMEM, pltpu.SMEM, pl.ANY))
    dma = pltpu.SemaphoreType.DMA
    arrived, slots = pl.pallas_call(
        kernel,
        out_shape=(
            jax.ShapeDtypeStruct((16 * CAP, T, T), bf16),
            jax.ShapeDtypeStruct((8, 128), jnp.int32),
        ),
        in_specs=[hbm, hbm, smem, smem, smem],
        out_specs=(hbm, vmem),
        scratch_shapes=[
            pltpu.VMEM((8, T, 4 * T), bf16),
            pltpu.VMEM((8, T, 4 * T), bf16),
            pltpu.VMEM((16, 8, T, 4 * T), bf16),
            pltpu.VMEM((8, 8, T, 4 * T), bf16),
            pltpu.VMEM((8 * PARTS[0][1], 4 * T), jnp.float32),
            pltpu.VMEM((32, T, T), bf16),
            [pltpu.VMEM((16 * CAP, hi - lo, T), bf16) for lo, hi in PARTS],
            pltpu.VMEM((16, 8, 128), jnp.int32),
            pltpu.VMEM((16, 8, 128), jnp.int32),
            pltpu.VMEM((1, 8, 128), jnp.int32),
            pltpu.SMEM((8, 128), jnp.int32),
            dma((320,)),
            dma((4, 2, PIECES)),
            dma((4, 2, PIECES)),
            dma((4, 2, PIECES)),
            dma((16,)),
            dma((len(PARTS), 16)),
            dma((2 + 2 * PIECES,)),
        ],
        compiler_params=pltpu.CompilerParams(
            collective_id=0, has_side_effects=True, vmem_limit_bytes=56 * 2**20
        ),
        cost_estimate=pl.CostEstimate(
            flops=2 * 1024 * 512 * 8192, bytes_accessed=4 * 2**20, transcendentals=0
        ),
    )(integrals.reshape(8, T, 4 * T), amplitudes.reshape(8, T, 4 * T), integral_tiles.T, amplitude_tiles.T, targets.T)
    return pl.pallas_call(
        unpack,
        out_shape=jax.ShapeDtypeStruct((1, 32, T, T), bf16),
        in_specs=[smem, vmem],
        out_specs=vmem,
    )(slots, arrived)


def solution(mesh):
    spec = P("row", "col")
    return jax.shard_map(
        on_device, mesh=mesh, in_specs=(spec,) * 5, out_specs=P("row", "col", None, None), check_vma=False
    )
```

```python
import functools

import jax
import jax.numpy as jnp
from jax import lax
from jax.experimental import pallas as pl
from jax.experimental.pallas import tpu as pltpu
from jax.sharding import PartitionSpec as P

MESH = pl.DeviceIdType.MESH
T = 128
CAP = 3
PIECES = 8
LATE = 1
SPREAD = [1, 15, 2, 14, 3, 13, 4, 12, 5, 11, 6, 10, 7, 9, 8]
PARTS = ((0, 32), (32, 80), (80, 128))


class Sems:
    def __init__(self, ref):
        self.ref, self.used = ref, 0

    def take(self):
        self.used += 1
        return self.ref.at[self.used - 1]


def halved(steps, dv, p):
    return LATE == 1 and steps in (1, 3) and dv == 1 and p == PIECES // 2 - 1


def forwards(steps, dv, p):
    return halved(steps, dv, p) or (steps == 1) == (p < PIECES // 2)


def arrival_order():
    queues = {(m, way): [] for m in "ab" for way in ("left", "right", "z")}
    left_over, order, halves = {key: 0.0 for key in queues}, [], set()
    for m in "ab":
        for p in own_order():
            queues[m, "left"].append((3, 0, p, 1))
            queues[m, "right"].append((1, 0, p, 1))
        for p in own_order():
            if p < PIECES - LATE:
                queues[m, "z"].append((0, 1, p, 1))
        for p in range(PIECES - LATE, PIECES):
            queues[m, "z"].append((0, 1, p, 1))
    while any(queues.values()):
        both = queues["a", "z"] and queues["b", "z"]
        for (m, way), queue in queues.items():
            if queue:
                left_over[m, way] += 0.0625 if way == "z" and both else 0.125
        for (m, way), queue in queues.items():
            if queue and left_over[m, way] >= queue[0][3]:
                left_over[m, way] = 0.0
                steps, dv, p, size = queue.pop(0)
                if size < 1 and (m, steps, dv, p) not in halves:
                    halves.add((m, steps, dv, p))
                    continue
                order.append((m, steps, dv, p))
                size = 0.5 if halved(steps, dv, p) else 1
                for how in onward(steps, dv, p):
                    if how == "z":
                        queues[m, "z"].append((steps, 1 - dv, p, 1))
                    elif how == "right":
                        queues[m, "right"].append((steps + 1, dv, p, size))
                    else:
                        queues[m, "left"].append(((steps + 3) % 4, dv, p, size))
    return order


def own_order():
    return [*range(PIECES - LATE, PIECES), *range(PIECES - LATE)]


def onward(steps, dv, p):
    late = p >= PIECES - LATE
    ways = []
    if steps == 0 and dv == 1 and not late:
        ways += ["left", "right"]
    if steps in (1, 3) and not (dv == 1 and late) and forwards(steps, dv, p):
        ways.append("right" if steps == 1 else "left")
    if dv == 0 and late and steps:
        ways.append("z")
    return ways


def kernel(
    a_hbm, b_hbm, a_tiles, b_tiles, targets, arrived, slots_ref,
    a_in, b_in, a_all, b_all, total, tiles, packed_parts, label_out, label_in, table, table_s,
    send_ref, recv_a, recv_s, recv_b, recv_h, recv_l, recv_d, local_sem,
):
    row, col = lax.axis_index("row"), lax.axis_index("col")
    y, zh = row // 2, row % 2
    x, zl, core = col // 4, (col // 2) % 2, col % 2
    sends = Sems(send_ref)
    started = []

    def col_of(dx, dv, dc):
        return lax.rem(x + dx + 4, 4) * 4 + lax.rem(zl + dv, 2) * 2 + lax.rem(core + dc, 2)

    def row_of(dy, dv):
        return lax.rem(y + dy + 4, 4) * 2 + lax.rem(zh + dv, 2)

    def send(src, dst, recv_sem, device):
        copy = pltpu.make_async_remote_copy(
            src_ref=src, dst_ref=dst, send_sem=sends.take(), recv_sem=recv_sem,
            device_id=device, device_id_type=MESH,
        )
        copy.start()
        started.append(copy)

    def landed(dst, recv_sem, device):
        pltpu.make_async_remote_copy(
            src_ref=dst, dst_ref=dst, send_sem=send_ref.at[0], recv_sem=recv_sem,
            device_id=device, device_id_type=MESH,
        ).wait_recv()

    barrier = pltpu.get_barrier_semaphore()
    peers = [(row, col_of(1, 0, 0)), (row, col_of(-1, 0, 0)), (row, col_of(0, 1, 0)), (row, col_of(0, 0, 1))]
    peers += [(row_of(1, 0), col), (row_of(-1, 0), col), (row_of(0, 1), col)]
    for peer in peers:
        pl.semaphore_signal(barrier, inc=1, device_id=peer, device_id_type=MESH)

    order = own_order()
    loads = []
    for n, p in enumerate(order):
        thin = pl.ds(p * 16, 16)
        loads.append((
            pltpu.make_async_copy(a_hbm.at[:, thin], a_in.at[:, thin], local_sem.at[2 + 2 * n]),
            pltpu.make_async_copy(b_hbm.at[p], b_in.at[p], local_sem.at[3 + 2 * n]),
        ))
        for load in loads[-1]:
            load.start()

    def mask(src, tile_flags, dst, i, rows):
        for j in range(4):
            flag = tile_flags[j, i].astype(jnp.float32)
            block = src[i, rows, pl.ds(j * T, T)].astype(jnp.float32) * flag
            dst[i, rows, pl.ds(j * T, T)] = block.astype(jnp.bfloat16)

    def a_piece(dx, dv, dc, p):
        return a_all.at[col_of(-dx, dv, dc), :, pl.ds(p * 16, 16)]

    def b_piece(dy, dv, p):
        return b_all.at[row_of(-dy, dv), p]

    def a_half(dx, dv, p, h):
        return a_all.at[col_of(-dx, dv, 0), pl.ds(4 * h, 4), pl.ds(p * 16, 16)]

    def b_half(dy, dv, p, h):
        return b_all.at[row_of(-dy, dv), p, pl.ds(T // 2 * h, T // 2)]

    def send_a(dx, dv, p, how):
        piece = a_piece(dx, dv, 0, p)
        if halved(dx, dv, p) and how in ("left", "right"):
            h, side = (0, 1) if how == "right" else (1, -1)
            send(a_half(dx, dv, p, h), a_half(dx, dv, p, h), recv_h.at[0, h], (row, col_of(side, 0, 0)))
            return
        if how == "right":
            send(piece, piece, recv_a.at[dx + 1, dv, p], (row, col_of(1, 0, 0)))
        elif how == "left":
            send(piece, piece, recv_a.at[(dx + 3) % 4, dv, p], (row, col_of(-1, 0, 0)))
        elif how == "z":
            send(piece, piece, recv_a.at[dx, 1 - dv, p], (row, col_of(0, 1, 0)))
        else:
            send(piece, piece, recv_s.at[dx, dv, p], (row, col_of(0, 0, 1)))

    def send_b(dy, dv, p, how):
        piece = b_piece(dy, dv, p)
        if halved(dy, dv, p) and how in ("left", "right"):
            h, side = (0, 1) if how == "right" else (1, -1)
            send(b_half(dy, dv, p, h), b_half(dy, dv, p, h), recv_h.at[1, h], (row_of(side, 0), col))
            return
        if how == "right":
            send(piece, piece, recv_b.at[dy + 1, dv, p], (row_of(1, 0), col))
        elif how == "left":
            send(piece, piece, recv_b.at[(dy + 3) % 4, dv, p], (row_of(-1, 0), col))
        else:
            send(piece, piece, recv_b.at[dy, 1 - dv, p], (row_of(0, 1), col))

    def got_s(dx, dv, p):
        landed(a_piece(dx, dv, 1, p), recv_s.at[dx, dv, p], (row, col_of(0, 0, 1)))

    mine_a, mine_b = a_all.at[col], b_all.at[row]
    for n, p in enumerate(order):
        late = p >= PIECES - LATE
        for load in loads[n]:
            load.wait()
        for i in range(8):
            mask(a_in, a_tiles, mine_a, i, pl.ds(p * 16, 16))
        mask(b_in, b_tiles, mine_b, p, pl.ds(0, T))
        if n == 0:
            pl.semaphore_wait(barrier, len(peers))
        for one in (send_a, send_b):
            if not late:
                one(0, 0, p, "z")
            one(0, 0, p, "left")
            one(0, 0, p, "right")
    for p in range(PIECES - LATE, PIECES):
        send_a(0, 0, p, "z")
        send_b(0, 0, p, "z")
    for p in order:
        send_a(0, 0, p, "core")

    at_tile = lax.broadcasted_iota(jnp.int32, (32, 128), 0)
    lane = lax.broadcasted_iota(jnp.int32, (32, 128), 1)
    target = jnp.zeros((32, 128), jnp.int32)
    for t in range(32):
        target = jnp.where(at_tile == t, targets[t % 4, t // 4], target)
    owner, slot = target // 32, target % 32
    rank = jnp.zeros((32, 128), jnp.int32)
    for t in range(32):
        rank += jnp.where((at_tile > t) & (owner == targets[t % 4, t // 4] // 32), 1, 0)
    place = owner * CAP + rank
    table[0] = jnp.broadcast_to(
        jnp.sum(jnp.where(place == lane, at_tile, 0), axis=0, keepdims=True), (8, 128)
    )
    for w in range(16):
        here = jnp.where((owner == w) & (slot == lane), col * CAP + rank + 1, 0)
        label_out[w] = jnp.broadcast_to(jnp.sum(here, axis=0, keepdims=True), (8, 128))
    copy = pltpu.make_async_copy(table.at[0], table_s, local_sem.at[0])
    copy.start()
    copy.wait()

    odd = lax.rem(x + y, 2)
    near, far = lax.rem(x + 1, 4), lax.rem(x + 3, 4)

    def dots(result, quarters, rows, k_tiles):
        count = rows[1] - rows[0]
        for quarter in quarters:
            for v in range(2):
                for c in range(2):
                    k = [t - 4 * c for t in k_tiles if t // 4 == c]
                    if not k:
                        continue
                    left = a_all[quarter * 4 + v * 2 + c, :, rows[0]:rows[1], k[0] * T:(k[-1] + 1) * T]
                    right = b_all[quarter * 2 + v, 4 * c + k[0]:4 * c + k[-1] + 1]
                    term = jnp.dot(
                        left.reshape(8 * count, len(k) * T), right.reshape(len(k) * T, 4 * T),
                        preferred_element_type=jnp.float32,
                    )
                    result = term if result is None else result + term
        return result

    early_quarters = ((near, far), (x, y))
    last_quarters = ((x, lax.rem(x + 2, 4)), (lax.rem(x + 2, 4), lax.rem(y + 2, 4)))

    def for_parity(step):
        for parity in range(2):
            @pl.when(odd == parity)
            def _():
                total[...] = step(early_quarters[parity], last_quarters[parity])

    todo = {(m, steps, dv, p) for m in "abs" for steps in range(4) for dv in range(2) for p in range(PIECES)}
    todo -= {(m, 0, 0, p) for p in range(PIECES) for m in "ab"}

    def of_part(part, steps):
        lo, hi = part
        return {("a", d, dv, p) for d in steps for dv in range(2) for p in range(lo // 16, hi // 16)}

    def need(part, steps):
        for _, d, dv, p in sorted(of_part(part, steps)):
            if ("s", d, dv, p) in todo:
                todo.discard(("s", d, dv, p))
                landed(a_piece(d, dv, 1, p), recv_s.at[d, dv, p], (row, col_of(0, 0, 1)))

    head, late_k = PARTS[0], range(PIECES - LATE, PIECES)
    early_k = range(PIECES - LATE)
    early_set = of_part(head, (0, 1, 3)) | {("b", d, dv, p) for d in (0, 1, 3) for dv in range(2) for p in early_k}
    early = False
    for m, steps, dv, p in arrival_order():
        todo.discard((m, steps, dv, p))
        if steps == 2 and halved(1, dv, p):
            for h in range(2):
                if m == "a":
                    landed(a_half(2, dv, p, h), recv_h.at[0, h], (row, col_of(0, 1, 0)))
                else:
                    landed(b_half(2, dv, p, h), recv_h.at[1, h], (row_of(0, 1), col))
        elif m == "a":
            landed(a_piece(steps, dv, 0, p), recv_a.at[steps, dv, p], (row, col_of(0, 1, 0)))
        else:
            landed(b_piece(steps, dv, p), recv_b.at[steps, dv, p], (row_of(0, 1), col))
        for how in onward(steps, dv, p):
            (send_a if m == "a" else send_b)(steps, dv, p, how)
        if m == "a":
            send_a(steps, dv, p, "core")
        if not early and not early_set & todo:
            early = True
            for d in range(1, 16):
                peer = lax.rem(col + d, 16)
                send(label_out.at[peer], label_in.at[col], recv_l.at[d], (row, peer))
            label_in[col] = label_out[col]
            need(head, (0, 1, 3))
            for_parity(lambda first, last: dots(None, first, head, early_k))

    stays = []
    for n, part in enumerate(PARTS):
        need(part, range(4))
        lo, hi = part
        if n == 0:
            for_parity(lambda first, last: dots(dots(total[...], first, part, late_k), last, part, range(8)))
            ladder = total[...]
        else:
            ladder = dots(None, range(4), part, range(8))
        ladder = ladder.astype(jnp.bfloat16).reshape(8, hi - lo, 4 * T)
        for i in range(8):
            for j in range(4):
                tiles[i * 4 + j, lo:hi] = ladder[i, :, j * T:(j + 1) * T]

        def pack(k, carry):
            packed_parts[n][k] = tiles[jnp.clip(table_s[0, k], 0, 31), lo:hi]
            return carry

        lax.fori_loop(0, 16 * CAP, pack, 0, unroll=4)
        rows = pl.ds(lo, hi - lo)
        for d in SPREAD:
            peer = lax.rem(col + d, 16)
            send(
                packed_parts[n].at[pl.ds(peer * CAP, CAP)], arrived.at[pl.ds(col * CAP, CAP), rows],
                recv_d.at[n, d], (row, peer),
            )
        stays.append(pltpu.make_async_copy(
            packed_parts[n].at[pl.ds(col * CAP, CAP)], arrived.at[pl.ds(col * CAP, CAP), rows],
            local_sem.at[2 + n],
        ))
        stays[-1].start()

    for d in range(1, 16):
        peer = lax.rem(col - d + 16, 16)
        landed(label_in.at[peer], recv_l.at[d], (row, peer))
    slots_ref[...] = jnp.clip(jnp.sum(label_in[...], axis=0) - 1, 0, 16 * CAP - 1)

    for n, (lo, hi) in enumerate(PARTS):
        rows = pl.ds(lo, hi - lo)
        stays[n].wait()
        for d in SPREAD:
            peer = lax.rem(col - d + 16, 16)
            landed(arrived.at[pl.ds(peer * CAP, CAP), rows], recv_d.at[n, d], (row, peer))
    for copy in started:
        copy.wait_send()


def unpack(slots, arrived, owned):
    def one(k, carry):
        owned[0, k] = arrived[slots[0, k]]
        return carry

    lax.fori_loop(0, 32, one, 0, unroll=4)


def on_device(integrals, amplitudes, integral_tiles, amplitude_tiles, targets):
    bf16 = jnp.bfloat16
    vmem, smem, hbm = (pl.BlockSpec(memory_space=s) for s in (pltpu.VMEM, pltpu.SMEM, pl.ANY))
    dma = pltpu.SemaphoreType.DMA
    arrived, slots = pl.pallas_call(
        kernel,
        out_shape=(
            jax.ShapeDtypeStruct((16 * CAP, T, T), bf16),
            jax.ShapeDtypeStruct((8, 128), jnp.int32),
        ),
        in_specs=[hbm, hbm, smem, smem, smem],
        out_specs=(hbm, vmem),
        scratch_shapes=[
            pltpu.VMEM((8, T, 4 * T), bf16),
            pltpu.VMEM((8, T, 4 * T), bf16),
            pltpu.VMEM((16, 8, T, 4 * T), bf16),
            pltpu.VMEM((8, 8, T, 4 * T), bf16),
            pltpu.VMEM((8 * PARTS[0][1], 4 * T), jnp.float32),
            pltpu.VMEM((32, T, T), bf16),
            [pltpu.VMEM((16 * CAP, hi - lo, T), bf16) for lo, hi in PARTS],
            pltpu.VMEM((16, 8, 128), jnp.int32),
            pltpu.VMEM((16, 8, 128), jnp.int32),
            pltpu.VMEM((1, 8, 128), jnp.int32),
            pltpu.SMEM((8, 128), jnp.int32),
            dma((320,)),
            dma((4, 2, PIECES)),
            dma((4, 2, PIECES)),
            dma((4, 2, PIECES)),
            dma((2, 2)),
            dma((16,)),
            dma((len(PARTS), 16)),
            dma((2 + 2 * PIECES,)),
        ],
        compiler_params=pltpu.CompilerParams(
            collective_id=0, has_side_effects=True, vmem_limit_bytes=56 * 2**20
        ),
        cost_estimate=pl.CostEstimate(
            flops=2 * 1024 * 512 * 8192, bytes_accessed=4 * 2**20, transcendentals=0
        ),
    )(integrals.reshape(8, T, 4 * T), amplitudes.reshape(8, T, 4 * T), integral_tiles.T, amplitude_tiles.T, targets.T)
    return pl.pallas_call(
        unpack,
        out_shape=jax.ShapeDtypeStruct((1, 32, T, T), bf16),
        in_specs=[smem, vmem],
        out_specs=vmem,
    )(slots, arrived)


def solution(mesh):
    spec = P("row", "col")
    return jax.shard_map(
        on_device, mesh=mesh, in_specs=(spec,) * 5, out_specs=P("row", "col", None, None), check_vma=False
    )
```

```python
import functools

import jax
import jax.numpy as jnp
from jax import lax
from jax.experimental import pallas as pl
from jax.experimental.pallas import tpu as pltpu
from jax.sharding import PartitionSpec as P

MESH = pl.DeviceIdType.MESH
T = 128
CAP = 3
PIECES = 8
LATE = 1
SPREAD = [1, 15, 2, 14, 3, 13, 4, 12, 5, 11, 6, 10, 7, 9, 8]
PARTS = ((0, 32), (32, 80), (80, 128))


class Sems:
    def __init__(self, ref):
        self.ref, self.used = ref, 0

    def take(self):
        self.used += 1
        return self.ref.at[self.used - 1]


def halved(steps, dv, p):
    return LATE == 1 and steps in (1, 3) and dv == 1 and p == PIECES // 2 - 1


def forwards(steps, dv, p):
    return halved(steps, dv, p) or (steps == 1) == (p < PIECES // 2)


def arrival_order():
    queues = {(m, way): [] for m in "ab" for way in ("left", "right", "z")}
    left_over, order, halves = {key: 0.0 for key in queues}, [], set()
    for m in "ab":
        for p in own_order():
            queues[m, "left"].append((3, 0, p, 1))
            queues[m, "right"].append((1, 0, p, 1))
        for p in own_order():
            if p < PIECES - LATE:
                queues[m, "z"].append((0, 1, p, 1))
        for p in range(PIECES - LATE, PIECES):
            queues[m, "z"].append((0, 1, p, 1))
    while any(queues.values()):
        both = queues["a", "z"] and queues["b", "z"]
        for (m, way), queue in queues.items():
            if queue:
                left_over[m, way] += 0.0625 if way == "z" and both else 0.125
        for (m, way), queue in queues.items():
            if queue and left_over[m, way] >= queue[0][3]:
                left_over[m, way] = 0.0
                steps, dv, p, size = queue.pop(0)
                if size < 1 and (m, steps, dv, p) not in halves:
                    halves.add((m, steps, dv, p))
                    continue
                order.append((m, steps, dv, p))
                size = 0.5 if halved(steps, dv, p) else 1
                for how in onward(steps, dv, p):
                    if how == "z":
                        queues[m, "z"].append((steps, 1 - dv, p, 1))
                    elif how == "right":
                        queues[m, "right"].append((steps + 1, dv, p, size))
                    else:
                        queues[m, "left"].append(((steps + 3) % 4, dv, p, size))
    return order


def own_order():
    return [*range(PIECES - LATE, PIECES), *range(PIECES - LATE)]


def onward(steps, dv, p):
    late = p >= PIECES - LATE
    ways = []
    if steps == 0 and dv == 1 and not late:
        ways += ["left", "right"]
    if steps in (1, 3) and not (dv == 1 and late) and forwards(steps, dv, p):
        ways.append("right" if steps == 1 else "left")
    if dv == 0 and late and steps:
        ways.append("z")
    return ways


def kernel(
    a_hbm, b_hbm, a_tiles, b_tiles, targets, arrived, slots_ref,
    a_in, b_in, a_all, b_all, total, tiles, packed_parts, label_out, label_in, table, table_s,
    send_ref, recv_a, recv_s, recv_b, recv_h, recv_l, recv_d, local_sem,
):
    row, col = lax.axis_index("row"), lax.axis_index("col")
    y, zh = row // 2, row % 2
    x, zl, core = col // 4, (col // 2) % 2, col % 2
    sends = Sems(send_ref)
    started = []

    def col_of(dx, dv, dc):
        return lax.rem(x + dx + 4, 4) * 4 + lax.rem(zl + dv, 2) * 2 + lax.rem(core + dc, 2)

    def row_of(dy, dv):
        return lax.rem(y + dy + 4, 4) * 2 + lax.rem(zh + dv, 2)

    def send(src, dst, recv_sem, device):
        copy = pltpu.make_async_remote_copy(
            src_ref=src, dst_ref=dst, send_sem=sends.take(), recv_sem=recv_sem,
            device_id=device, device_id_type=MESH,
        )
        copy.start()
        started.append(copy)

    def landed(dst, recv_sem, device):
        pltpu.make_async_remote_copy(
            src_ref=dst, dst_ref=dst, send_sem=send_ref.at[0], recv_sem=recv_sem,
            device_id=device, device_id_type=MESH,
        ).wait_recv()

    barrier = pltpu.get_barrier_semaphore()
    peers = [(row, col_of(1, 0, 0)), (row, col_of(-1, 0, 0)), (row, col_of(0, 1, 0)), (row, col_of(0, 0, 1))]
    peers += [(row_of(1, 0), col), (row_of(-1, 0), col), (row_of(0, 1), col)]
    for peer in peers:
        pl.semaphore_signal(barrier, inc=1, device_id=peer, device_id_type=MESH)

    order = own_order()
    loads = []
    for n, p in enumerate(order):
        thin = pl.ds(p * 16, 16)
        loads.append((
            pltpu.make_async_copy(a_hbm.at[:, thin], a_in.at[:, thin], local_sem.at[2 + 2 * n]),
            pltpu.make_async_copy(b_hbm.at[p], b_in.at[p], local_sem.at[3 + 2 * n]),
        ))
        for load in loads[-1]:
            load.start()

    def mask(src, tile_flags, dst, i, rows):
        for j in range(4):
            flag = tile_flags[j, i].astype(jnp.float32)
            block = src[i, rows, pl.ds(j * T, T)].astype(jnp.float32) * flag
            dst[i, rows, pl.ds(j * T, T)] = block.astype(jnp.bfloat16)

    def a_piece(dx, dv, dc, p):
        return a_all.at[col_of(-dx, dv, dc), :, pl.ds(p * 16, 16)]

    def b_piece(dy, dv, p):
        return b_all.at[row_of(-dy, dv), p]

    def a_half(dx, dv, p, h):
        return a_all.at[col_of(-dx, dv, 0), pl.ds(4 * h, 4), pl.ds(p * 16, 16)]

    def b_half(dy, dv, p, h):
        return b_all.at[row_of(-dy, dv), p, pl.ds(T // 2 * h, T // 2)]

    def send_a(dx, dv, p, how):
        piece = a_piece(dx, dv, 0, p)
        if halved(dx, dv, p) and how in ("left", "right"):
            h, side = (0, 1) if how == "right" else (1, -1)
            send(a_half(dx, dv, p, h), a_half(dx, dv, p, h), recv_h.at[0, h], (row, col_of(side, 0, 0)))
            return
        if how == "right":
            send(piece, piece, recv_a.at[dx + 1, dv, p], (row, col_of(1, 0, 0)))
        elif how == "left":
            send(piece, piece, recv_a.at[(dx + 3) % 4, dv, p], (row, col_of(-1, 0, 0)))
        elif how == "z":
            send(piece, piece, recv_a.at[dx, 1 - dv, p], (row, col_of(0, 1, 0)))
        else:
            send(piece, piece, recv_s.at[dx, dv, p], (row, col_of(0, 0, 1)))

    def send_b(dy, dv, p, how):
        piece = b_piece(dy, dv, p)
        if halved(dy, dv, p) and how in ("left", "right"):
            h, side = (0, 1) if how == "right" else (1, -1)
            send(b_half(dy, dv, p, h), b_half(dy, dv, p, h), recv_h.at[1, h], (row_of(side, 0), col))
            return
        if how == "right":
            send(piece, piece, recv_b.at[dy + 1, dv, p], (row_of(1, 0), col))
        elif how == "left":
            send(piece, piece, recv_b.at[(dy + 3) % 4, dv, p], (row_of(-1, 0), col))
        else:
            send(piece, piece, recv_b.at[dy, 1 - dv, p], (row_of(0, 1), col))

    def got_s(dx, dv, p):
        landed(a_piece(dx, dv, 1, p), recv_s.at[dx, dv, p], (row, col_of(0, 0, 1)))

    mine_a, mine_b = a_all.at[col], b_all.at[row]
    for n, p in enumerate(order):
        late = p >= PIECES - LATE
        for load in loads[n]:
            load.wait()
        for i in range(8):
            mask(a_in, a_tiles, mine_a, i, pl.ds(p * 16, 16))
        mask(b_in, b_tiles, mine_b, p, pl.ds(0, T))
        if n == 0:
            pl.semaphore_wait(barrier, len(peers))
        for one in (send_a, send_b):
            if not late:
                one(0, 0, p, "z")
            one(0, 0, p, "left")
            one(0, 0, p, "right")
    for p in range(PIECES - LATE, PIECES):
        send_a(0, 0, p, "z")
        send_b(0, 0, p, "z")
    for p in order:
        send_a(0, 0, p, "core")

    at_tile = lax.broadcasted_iota(jnp.int32, (32, 128), 0)
    lane = lax.broadcasted_iota(jnp.int32, (32, 128), 1)
    target = jnp.zeros((32, 128), jnp.int32)
    for t in range(32):
        target = jnp.where(at_tile == t, targets[t % 4, t // 4], target)
    owner, slot = target // 32, target % 32
    rank = jnp.zeros((32, 128), jnp.int32)
    for t in range(32):
        rank += jnp.where((at_tile > t) & (owner == targets[t % 4, t // 4] // 32), 1, 0)
    place = owner * CAP + rank
    table[0] = jnp.broadcast_to(
        jnp.sum(jnp.where(place == lane, at_tile, 0), axis=0, keepdims=True), (8, 128)
    )
    for w in range(16):
        here = jnp.where((owner == w) & (slot == lane), col * CAP + rank + 1, 0)
        label_out[w] = jnp.broadcast_to(jnp.sum(here, axis=0, keepdims=True), (8, 128))
    copy = pltpu.make_async_copy(table.at[0], table_s, local_sem.at[0])
    copy.start()
    copy.wait()

    odd = lax.rem(x + y, 2)
    near, far = lax.rem(x + 1, 4), lax.rem(x + 3, 4)

    def dots(result, quarters, rows, k_tiles):
        count = rows[1] - rows[0]
        for quarter in quarters:
            for v in range(2):
                for c in range(2):
                    k = [t - 4 * c for t in k_tiles if t // 4 == c]
                    if not k:
                        continue
                    left = a_all[quarter * 4 + v * 2 + c, :, rows[0]:rows[1], k[0] * T:(k[-1] + 1) * T]
                    right = b_all[quarter * 2 + v, 4 * c + k[0]:4 * c + k[-1] + 1]
                    term = jnp.dot(
                        left.reshape(8 * count, len(k) * T), right.reshape(len(k) * T, 4 * T),
                        preferred_element_type=jnp.float32,
                    )
                    result = term if result is None else result + term
        return result

    early_quarters = ((near, far), (x, y))
    last_quarters = ((x, lax.rem(x + 2, 4)), (lax.rem(x + 2, 4), lax.rem(y + 2, 4)))

    def for_parity(step):
        for parity in range(2):
            @pl.when(odd == parity)
            def _():
                total[...] = step(early_quarters[parity], last_quarters[parity])

    todo = {(m, steps, dv, p) for m in "abs" for steps in range(4) for dv in range(2) for p in range(PIECES)}
    todo -= {(m, 0, 0, p) for p in range(PIECES) for m in "ab"}

    def of_part(part, steps):
        lo, hi = part
        return {("a", d, dv, p) for d in steps for dv in range(2) for p in range(lo // 16, hi // 16)}

    def need(part, steps):
        for _, d, dv, p in sorted(of_part(part, steps)):
            if ("s", d, dv, p) in todo:
                todo.discard(("s", d, dv, p))
                landed(a_piece(d, dv, 1, p), recv_s.at[d, dv, p], (row, col_of(0, 0, 1)))

    head, late_k = PARTS[0], range(PIECES - LATE, PIECES)
    early_k = range(PIECES - LATE)
    early_set = of_part(head, (0, 1, 3)) | {("b", d, dv, p) for d in (0, 1, 3) for dv in range(2) for p in early_k}
    soon_k, rest_k = (0, 1, 4), (2, 3, 5, 6, 7)
    soon_set = of_part(head, range(4)) | {("b", 2, dv, p) for dv in range(2) for p in soon_k}
    soon_set |= {("b", d, dv, p) for d in (0, 1, 3) for dv in range(2) for p in range(PIECES)}
    early = soon = False
    for m, steps, dv, p in arrival_order():
        todo.discard((m, steps, dv, p))
        if steps == 2 and halved(1, dv, p):
            for h in range(2):
                if m == "a":
                    landed(a_half(2, dv, p, h), recv_h.at[0, h], (row, col_of(0, 1, 0)))
                else:
                    landed(b_half(2, dv, p, h), recv_h.at[1, h], (row_of(0, 1), col))
        elif m == "a":
            landed(a_piece(steps, dv, 0, p), recv_a.at[steps, dv, p], (row, col_of(0, 1, 0)))
        else:
            landed(b_piece(steps, dv, p), recv_b.at[steps, dv, p], (row_of(0, 1), col))
        for how in onward(steps, dv, p):
            (send_a if m == "a" else send_b)(steps, dv, p, how)
        if m == "a":
            send_a(steps, dv, p, "core")
        if not early and not early_set & todo:
            early = True
            for d in range(1, 16):
                peer = lax.rem(col + d, 16)
                send(label_out.at[peer], label_in.at[col], recv_l.at[d], (row, peer))
            label_in[col] = label_out[col]
            need(head, (0, 1, 3))
            for_parity(lambda first, last: dots(None, first, head, early_k))
        if early and not soon and not soon_set & todo:
            soon = True
            need(head, (2,))
            for_parity(lambda first, last: dots(dots(total[...], first, head, late_k), last, head, soon_k))

    stays = []
    for n, part in enumerate(PARTS):
        need(part, range(4))
        lo, hi = part
        if n == 0:
            for_parity(lambda first, last: dots(total[...], last, part, rest_k))
            ladder = total[...]
        else:
            ladder = dots(None, range(4), part, range(8))
        ladder = ladder.astype(jnp.bfloat16).reshape(8, hi - lo, 4 * T)
        for i in range(8):
            for j in range(4):
                tiles[i * 4 + j, lo:hi] = ladder[i, :, j * T:(j + 1) * T]

        def pack(k, carry):
            packed_parts[n][k] = tiles[jnp.clip(table_s[0, k], 0, 31), lo:hi]
            return carry

        lax.fori_loop(0, 16 * CAP, pack, 0, unroll=4)
        rows = pl.ds(lo, hi - lo)
        for d in SPREAD:
            peer = lax.rem(col + d, 16)
            send(
                packed_parts[n].at[pl.ds(peer * CAP, CAP)], arrived.at[pl.ds(col * CAP, CAP), rows],
                recv_d.at[n, d], (row, peer),
            )
        stays.append(pltpu.make_async_copy(
            packed_parts[n].at[pl.ds(col * CAP, CAP)], arrived.at[pl.ds(col * CAP, CAP), rows],
            local_sem.at[2 + n],
        ))
        stays[-1].start()

    for d in range(1, 16):
        peer = lax.rem(col - d + 16, 16)
        landed(label_in.at[peer], recv_l.at[d], (row, peer))
    slots_ref[...] = jnp.clip(jnp.sum(label_in[...], axis=0) - 1, 0, 16 * CAP - 1)

    for n, (lo, hi) in enumerate(PARTS):
        rows = pl.ds(lo, hi - lo)
        stays[n].wait()
        for d in SPREAD:
            peer = lax.rem(col - d + 16, 16)
            landed(arrived.at[pl.ds(peer * CAP, CAP), rows], recv_d.at[n, d], (row, peer))
    for copy in started:
        copy.wait_send()


def unpack(slots, arrived, owned):
    def one(k, carry):
        owned[0, k] = arrived[slots[0, k]]
        return carry

    lax.fori_loop(0, 32, one, 0, unroll=4)


def on_device(integrals, amplitudes, integral_tiles, amplitude_tiles, targets):
    bf16 = jnp.bfloat16
    vmem, smem, hbm = (pl.BlockSpec(memory_space=s) for s in (pltpu.VMEM, pltpu.SMEM, pl.ANY))
    dma = pltpu.SemaphoreType.DMA
    arrived, slots = pl.pallas_call(
        kernel,
        out_shape=(
            jax.ShapeDtypeStruct((16 * CAP, T, T), bf16),
            jax.ShapeDtypeStruct((8, 128), jnp.int32),
        ),
        in_specs=[hbm, hbm, smem, smem, smem],
        out_specs=(hbm, vmem),
        scratch_shapes=[
            pltpu.VMEM((8, T, 4 * T), bf16),
            pltpu.VMEM((8, T, 4 * T), bf16),
            pltpu.VMEM((16, 8, T, 4 * T), bf16),
            pltpu.VMEM((8, 8, T, 4 * T), bf16),
            pltpu.VMEM((8 * PARTS[0][1], 4 * T), jnp.float32),
            pltpu.VMEM((32, T, T), bf16),
            [pltpu.VMEM((16 * CAP, hi - lo, T), bf16) for lo, hi in PARTS],
            pltpu.VMEM((16, 8, 128), jnp.int32),
            pltpu.VMEM((16, 8, 128), jnp.int32),
            pltpu.VMEM((1, 8, 128), jnp.int32),
            pltpu.SMEM((8, 128), jnp.int32),
            dma((320,)),
            dma((4, 2, PIECES)),
            dma((4, 2, PIECES)),
            dma((4, 2, PIECES)),
            dma((2, 2)),
            dma((16,)),
            dma((len(PARTS), 16)),
            dma((2 + 2 * PIECES,)),
        ],
        compiler_params=pltpu.CompilerParams(
            collective_id=0, has_side_effects=True, vmem_limit_bytes=56 * 2**20
        ),
        cost_estimate=pl.CostEstimate(
            flops=2 * 1024 * 512 * 8192, bytes_accessed=4 * 2**20, transcendentals=0
        ),
    )(integrals.reshape(8, T, 4 * T), amplitudes.reshape(8, T, 4 * T), integral_tiles.T, amplitude_tiles.T, targets.T)
    return pl.pallas_call(
        unpack,
        out_shape=jax.ShapeDtypeStruct((1, 32, T, T), bf16),
        in_specs=[smem, vmem],
        out_specs=vmem,
    )(slots, arrived)


def solution(mesh):
    spec = P("row", "col")
    return jax.shard_map(
        on_device, mesh=mesh, in_specs=(spec,) * 5, out_specs=P("row", "col", None, None), check_vma=False
    )
```
